128 devices in a mesh: wide: 32 (over z, y, core), narrow: 4 (over x).
Axes of the slice: x: 4, y: 4, z: 4, core: 2. Of those that a mesh axis runs over, the one named last changes fastest.
Arguments:
- factors: bfloat16 [15, 7168, 1920], P(None, ('wide', 'narrow')), may hold values from -0.625 to 0.625
- t2_window: bfloat16 [16, 15, 15], replicated, may hold values from -0.3984375 to 0.3984375
- residual_in: bfloat16 [256, 16, 16384], P('wide', 'narrow'), may hold values from -6 to 6
- tile_mask: int32 [225], replicated, may hold values from 0 to 1, as said below
- owner_slot: int32 [225], replicated, may hold values from 0 to 63, as said below
- home_slot: int32 [225], replicated, may hold values from 0 to 255, as said below
Outputs:
- residual_out: bfloat16 [256, 16, 16384], P('wide', 'narrow')
- ladder_norms: float32 [64, 16], P('wide', 'narrow')
The draws below stay inside these ranges and needn't reach their ends.
Inputs may be any that keep to these rules, and one draw needn't show every extreme that they name: `tile_mask`: exactly 64 tiles are filled. `owner_slot`: the filled tiles take the owner slots 0 to 63, one each; slot o belongs to wide index o // 2; the filled tiles of one wide index have different home wide indices. Entries of tiles that are not filled mean nothing. `home_slot`: all different; home slot s lies on wide index s // 8.
All inputs are finite; a program needn't handle non-finite values.
Results may differ from the reference program's by a relative error of at most 0.0045.
Values may be sent and summed in bfloat16 or wider, within the bound.
A program may use at most 192 MiB of HBM per device.

```python
import jax
import jax.numpy as jnp
from jax import lax

VT = 128
NAUX = 7168
W = 15
SLOTS = 2
NC = 15
NT = 225
WVT = 1920
NP = 16
FILLED = 64
HOME_DEV = 8
HOMES = 256
N_WIDE = 32


def plan_tiles(key):
    key_home, key_fill, key_owner, key_spare = jax.random.split(key, 4)
    home_raw = jax.random.permutation(key_home, HOMES)[:NT].astype(jnp.int32)
    home_slot = jnp.where(home_raw == jnp.max(home_raw), HOMES - 1, home_raw)
    home_slot = jnp.where(home_raw == jnp.min(home_raw), 0, home_slot)
    usable = home_slot % HOME_DEV < min(HOME_DEV, N_WIDE)
    fill_rank = jax.random.permutation(key_fill, NT).astype(jnp.int32)
    fill_order = jnp.argsort(jnp.where(usable, 0, NT) + fill_rank)
    tile_mask = jnp.zeros((NT,), jnp.int32).at[fill_order[:FILLED]].set(1)
    tile_ids = jnp.arange(NT, dtype=jnp.int32)
    sort_key = jnp.where(tile_mask == 1, home_slot // HOME_DEV * NT + tile_ids, HOMES * NT + tile_ids)
    by_home = jnp.argsort(sort_key)
    position = jnp.zeros((NT,), jnp.int32).at[by_home].set(tile_ids)
    owner_order = jax.random.permutation(key_owner, N_WIDE).astype(jnp.int32)
    assigned = owner_order[position % N_WIDE] * SLOTS + position // N_WIDE
    spare_slot = jax.random.randint(key_spare, (NT,), 0, FILLED, dtype=jnp.int32)
    owner_slot = jnp.where(tile_mask == 1, assigned, spare_slot)
    return (tile_mask, owner_slot, home_slot)


def draw_tile_mask(key, part):
    shared = plan_tiles(key)
    return shared[0]


def draw_owner_slot(key, part):
    shared = plan_tiles(key)
    return shared[1]


def draw_home_slot(key, part):
    shared = plan_tiles(key)
    return shared[2]


def block_levels(stream_key, dims, cuts, smallest, largest):
    gain, own = 1.0, jax.random.fold_in(stream_key, 6)
    for dim, blocks in cuts:
        steps = jnp.exp(jax.random.uniform(jax.random.fold_in(own, dim), (blocks,), jnp.float32, smallest / len(cuts), largest / len(cuts)))
        gain = gain * jnp.repeat(steps, dims[dim] // blocks).reshape([-1 if axis == dim else 1 for axis in range(len(dims))])
    return gain


def bell_draw(key, shape, width, limit, pieces=(), held_as=jnp.bfloat16):
    array = width * jax.random.normal(key, shape, jnp.float32)
    if pieces:
        array = array * block_levels(key, shape, pieces, -0.22, 0.18)
    return jnp.clip(array, -limit, limit).astype(held_as)


def setup_inputs(seed: int = 0) -> dict:
    key_of = jax.random.split(jax.random.key(seed), 7)
    factors = bell_draw(key_of[0], (NC, NAUX, WVT), (NAUX ** 0.5) ** -0.5, 0.625, ((1, 128),))
    t2_window = bell_draw(key_of[1], (NP, W, W), (W ** -1), 0.3984375)
    residual_in = bell_draw(key_of[2], (HOMES, NP, VT * VT), 1.0, 6.0, ((0, 32), (1, 4)))
    tile_mask = draw_tile_mask(jax.random.fold_in(key_of[6], 71), 0)
    owner_slot = draw_owner_slot(jax.random.fold_in(key_of[6], 71), 0)
    home_slot = draw_home_slot(jax.random.fold_in(key_of[6], 71), 0)
    return dict(factors=factors, t2_window=t2_window, residual_in=residual_in, tile_mask=tile_mask, owner_slot=owner_slot, home_slot=home_slot)


def tile_ladder(factors, amplitude, tile):
    clusters = factors.shape[0]
    window = amplitude.shape[1]
    tile_width = factors.shape[2] // window
    first_side = lax.dynamic_index_in_dim(factors, tile // clusters, 0, keepdims=False)
    second_side = lax.dynamic_index_in_dim(factors, tile % clusters, 0, keepdims=False)
    integral = jnp.dot(first_side.T, second_side, preferred_element_type=jnp.float32)
    summed = jnp.einsum("cadb,pcd->pab", integral.reshape(window, tile_width, window, tile_width), amplitude, precision=lax.Precision.HIGHEST)
    return summed.reshape(amplitude.shape[0], tile_width * tile_width).astype(jnp.bfloat16)


def reference(factors, t2_window, residual_in, tile_mask, owner_slot, home_slot):
    amplitude = t2_window.astype(jnp.float32)
    tile_ids = jnp.arange(NT, dtype=jnp.int32)
    is_filled = tile_mask == 1
    owner_match = is_filled[:, None] & (owner_slot[:, None] == jnp.arange(FILLED, dtype=jnp.int32)[None, :])
    tile_of_slot = jnp.sum(jnp.where(owner_match, tile_ids[:, None], 0), axis=0).astype(jnp.int32)
    ladders = lax.map(lambda tile: tile_ladder(factors, amplitude, tile), tile_of_slot)
    ladder_wide = ladders.astype(jnp.float32)
    ladder_norms = jnp.mean(ladder_wide * ladder_wide, axis=2)
    present = is_filled[:, None] & (home_slot[:, None] == jnp.arange(HOMES, dtype=jnp.int32)[None, :])
    kept_slot = jnp.any(present, axis=0)
    source_slot = jnp.sum(jnp.where(present, owner_slot[:, None], 0), axis=0).astype(jnp.int32)
    picked = jnp.take(ladders, source_slot, axis=0).astype(jnp.float32)
    combined = residual_in.astype(jnp.float32) + picked
    residual_out = jnp.where(kept_slot[:, None, None], combined, 0.0).astype(jnp.bfloat16)
    return residual_out, ladder_norms
```

```python
import functools

import jax
import jax.numpy as jnp
from jax import lax
from jax.experimental import pallas as pl
from jax.experimental.pallas import tpu as pltpu
from jax.sharding import PartitionSpec as P

BF = jnp.bfloat16
F32 = jnp.float32
MESH = pl.DeviceIdType.MESH
VT = 128
W = 15
NC = 15
ROWS = 56
KC = 1792
FILLED = 64


def place():
    w = lax.axis_index("wide")
    return lax.axis_index("narrow"), (w // 2) % 4, w // 8, w % 2


def at(x, y, z, c):
    return {"wide": z * 8 + y * 2 + c, "narrow": x}


def ladder_kernel(
    first, second, amp, own_rows,
    spread, other_rows,
    weights, f2, f1t, y_buf, out, raw, rx, ry, rz, r2, r3,
    ex_s, ex_r, ld_s, x_s, x_r, y_s, y_r, z_s, z_r, s2_s, s2_r, s3_s, s3_r, ag_s, ag_r, co_s, co_r, st_s,
):
    x, y, z, c = place()
    ring = {
        "x": (x, at((x + 1) % 4, y, z, c), at((x + 3) % 4, y, z, c)),
        "y": (y, at(x, (y + 1) % 4, z, c), at(x, (y + 3) % 4, z, c)),
        "z": (z, at(x, y, (z + 1) % 4, c), at(x, y, (z + 3) % 4, c)),
    }
    partner = at(x, y, z, 1 - c)

    barrier = pltpu.get_barrier_semaphore()
    greeted = [partner] + [ring[a][i] for a in "xyz" for i in (1, 2)]
    for device in greeted:
        pl.semaphore_signal(barrier, inc=1, device_id=device, device_id_type=MESH)
    pl.semaphore_wait(barrier, len(greeted))

    def remote(src, dst, s_sem, r_sem, device):
        return pltpu.make_async_remote_copy(
            src_ref=src, dst_ref=dst, send_sem=s_sem, recv_sem=r_sem, device_id=device, device_id_type=MESH
        )

    def exchange(i):
        return remote(own_rows.at[i], other_rows.at[i], ex_s.at[i], ex_r.at[i], partner)

    def start_exchange(i, _):
        exchange(i).start()
        return 0

    lax.fori_loop(0, NC, start_exchange, 0)

    row = lax.broadcasted_iota(jnp.int32, (256, 16), 0)
    col = lax.broadcasted_iota(jnp.int32, (256, 16), 1)
    widen = (row // 16 == col).astype(F32).astype(BF)
    row2 = lax.broadcasted_iota(jnp.int32, (256, 256), 0)
    col2 = lax.broadcasted_iota(jnp.int32, (256, 256), 1)
    same = row2 % 16 == col2 % 16
    for i in range(8):
        tall = jnp.dot(widen, amp[i], preferred_element_type=F32).astype(BF)
        full = lax.dot_general(tall, widen, (((1,), (1,)), ((), ())), preferred_element_type=F32)
        weights[i // 2, (i % 2) * 256:(i % 2) * 256 + 256, :] = jnp.where(same, full, 0.0).astype(BF)

    def load(which, i):
        src = (own_rows, other_rows)[which]
        return pltpu.make_async_copy(src.at[i], raw.at[which, i % 2], ld_s.at[which, i % 2])

    def start_load(i):
        load(0, i).start()
        exchange(i).wait_recv()
        load(1, i).start()

    start_load(0)
    f2[52, :, 128:256] = jnp.zeros((256, 128), BF)

    def assemble(i, _):
        @pl.when(i + 1 < NC)
        def _():
            start_load(i + 1)

        load(0, i).wait()
        load(1, i).wait()
        slot = i % 2
        for blk in range(7):
            parts = []
            for d in range(W):
                lanes = slice(d * 128, d * 128 + 128)
                if blk < 6:
                    r0 = (blk % 3) * 16
                    parts.append(raw[blk // 3, slot, r0:r0 + 16, lanes])
                else:
                    parts.append(
                        jnp.concatenate([raw[0, slot, 48:56, lanes], raw[1, slot, 48:56, lanes]], axis=0)
                    )
            parts.append(jnp.zeros((16, 128), BF))
            block = jnp.concatenate(parts, axis=0)
            f1t[i, :, blk * 256:blk * 256 + 256] = block.T
            if blk < 6:
                f2[i * 3 + blk // 2, :, (blk % 2) * 128:(blk % 2) * 128 + 128] = block
            else:
                f2[45 + i // 2, :, pl.ds(pl.multiple_of((i % 2) * 128, 128), 128)] = block
        return 0

    lax.fori_loop(0, NC, assemble, 0)

    def put(axis, view, recv, s_sem, r_sem, way, kind):
        step = 2 if kind == 0 else (1 if way == 0 else 3)
        half = {0: way, 1: 1 - way, 2: way}[kind]
        return remote(view(step, half), recv(way, kind), s_sem(way, kind), r_sem(way, kind), ring[axis][1 + way])

    def add_tiles(dst, terms, n):
        def one(i, _):
            total = dst.at[i][...].astype(F32)
            for term in terms:
                total = total + term.at[i][...].astype(F32)
            dst.at[i][...] = total.astype(BF)
            return 0

        lax.fori_loop(0, n, one, 0)

    def view1(axis, s):
        coord, base = ring[axis][0], 32 if axis == "y" else 48
        return lambda k, h: out.at[s, :, pl.ds(base + ((coord + k) % 4) * 4 + 2 * h, 2)]

    def put1(axis, s, way, kind):
        buf, ss, rs = (ry, y_s, y_r) if axis == "y" else (rz, z_s, z_r)
        return put(
            axis, view1(axis, s), lambda w, k: buf.at[w, k, s], lambda w, k: ss.at[s, w, k],
            lambda w, k: rs.at[s, w, k], way, kind,
        )

    def later1(axis, s):
        buf = ry if axis == "y" else rz
        for way in (0, 1):
            put1(axis, s, way, 0).wait_recv()
            dst = view1(axis, s)(1 if way == 0 else 3, way)
            for slot in range(2):
                add_tiles(dst.at[slot], [buf.at[way, 0, s, slot]], 2)
            put1(axis, s, way, 2).start()

    X_AT = {(0, 0): (0, 0), (1, 0): (0, 1), (0, 1): (1, 0), (1, 1): (1, 1), (0, 2): (2, 0), (1, 2): (2, 1)}

    def put_x(b, way, kind):
        s, slot = X_AT[(way, kind)]
        return remote(
            out.at[s, slot, b * 16:b * 16 + 16], rx.at[b, way, kind], x_s.at[b, way, kind], x_r.at[b, way, kind],
            ring["x"][1 + way],
        )

    def compute(s, b):
        def group(i, _):
            for u in range(8):
                t = b * 16 + i * 8 + u
                o = jnp.dot(f1t[first[t]], y_buf[second[t]], preferred_element_type=F32).astype(BF)
                out[s, 0, t] = o[:, :128]
                out[s, 1, t] = o[:, 128:]
            return 0

        lax.fori_loop(0, 2, group, 0)

    def amplitudes(s):
        def put_block(o, i, blk, half):
            rows = slice(blk * 256, blk * 256 + 256)
            for slot in range(2):
                y_buf[i, rows, slot * 128:slot * 128 + 128] = o[slot * 256:slot * 256 + 256, half * 128:half * 128 + 128]

        def cluster(i, _):
            for j in range(3):
                o = jnp.dot(weights[s], f2[i * 3 + j], preferred_element_type=F32).astype(BF)
                for half in range(2):
                    put_block(o, i, 2 * j + half, half)
            return 0

        lax.fori_loop(0, NC, cluster, 0)

        def tail(i, _):
            o = jnp.dot(weights[s], f2[45 + i], preferred_element_type=F32).astype(BF)
            for half in range(2):
                put_block(o, 2 * i + half, 6, half)
            return 0

        lax.fori_loop(0, 7, tail, 0)
        o = jnp.dot(weights[s], f2[52], preferred_element_type=F32).astype(BF)
        put_block(o, 14, 6, 0)

    def step(s, _):
        amplitudes(s)
        for b in (0, 1):
            compute(s, b)

            @pl.when(s == 0)
            def _():
                for way in (0, 1):
                    put_x(b, way, 0).start()

            @pl.when(s == 1)
            def _():
                for way in (0, 1):
                    put_x(b, way, 1).start()

            @pl.when(s == 2)
            def _():
                for way in (0, 1):
                    put_x(b, way, 0).wait_recv()
                    add_tiles(out.at[2, way, b * 16:b * 16 + 16], [rx.at[b, way, 0]], 16)
                    put_x(b, way, 2).start()

        for b, axis in ((2, "y"), (3, "z")):
            compute(s, b)
            for kind in (0, 1):
                for way in (0, 1):
                    put1(axis, s, way, kind).start()

            @pl.when(s >= 1)
            def _():
                later1(axis, s - 1)
        return 0

    lax.fori_loop(0, 4, step, 0)

    def stage(axis, view, recv, sems, n):
        def one(way, kind):
            return put(axis, view, recv, lambda w, k: sems[0].at[w, k], lambda w, k: sems[1].at[w, k], way, kind)

        for kind in (0, 1):
            for way in (0, 1):
                one(way, kind).start()
        yield
        for way in (0, 1):
            one(way, 0).wait_recv()
            add_tiles(view(1 if way == 0 else 3, way), [recv(way, 0)], n)
            one(way, 2).start()
        yield
        for kind in (1, 2):
            for way in (0, 1):
                one(way, kind).wait_recv()
        add_tiles(view(0, 0), [recv(0, 2), recv(1, 1)], n)
        add_tiles(view(0, 1), [recv(0, 1), recv(1, 2)], n)

    mine = pl.ds(2 * c, 2)

    def gather(axis, block, own, sems):
        def copy(i):
            way = i % 2
            if i < 2:
                src = own
                dst = spread.at[mine, block(0)]
            else:
                k = 3 if way == 0 else 1
                src = spread.at[2 * c + way, block(k)]
                dst = src
            return remote(src, dst, sems[0].at[i], sems[1].at[i], ring[axis][1 + way])

        copy(0).start()
        copy(1).start()
        yield
        copy(0).wait_recv()
        copy(2).start()
        copy(1).wait_recv()
        copy(3).start()
        yield
        copy(2).wait_recv()
        copy(3).wait_recv()

    def batch(b):
        base = 16 * b
        major = "y" if b in (0, 2) else "z"
        minor = "z" if major == "y" else "y"
        hi, lo = ring[major][0], ring[minor][0]
        if b < 2:
            for way in (0, 1):
                for kind in (1, 2):
                    put_x(b, way, kind).wait_recv()
            add_tiles(out.at[3, 0, base:base + 16], [rx.at[b, 0, 2], rx.at[b, 1, 1]], 16)
            add_tiles(out.at[3, 1, base:base + 16], [rx.at[b, 0, 1], rx.at[b, 1, 2]], 16)
            yield
            yield from stage(
                major, lambda k, h: out.at[3, h, pl.ds(base + ((hi + k) % 4) * 4, 4)],
                lambda w, k: r2.at[b, w, k], (s2_s.at[b], s2_r.at[b]), 4,
            )
            yield
            yield from stage(
                minor, lambda k, h: out.at[3, h, pl.ds(base + hi * 4 + (lo + k) % 4, 1)],
                lambda w, k: r3.at[b, w, k], (s3_s.at[b], s3_r.at[b]), 1,
            )
        else:
            buf = ry if b == 2 else rz
            later1(major, 3)
            yield
            for s in range(4):
                for way in (0, 1):
                    for kind in (1, 2):
                        put1(major, s, way, kind).wait_recv()
                for slot in range(2):
                    own = lambda h: out.at[s, slot, pl.ds(base + hi * 4 + 2 * h, 2)]
                    add_tiles(own(0), [buf.at[0, 2, s, slot], buf.at[1, 1, s, slot]], 2)
                    add_tiles(own(1), [buf.at[0, 1, s, slot], buf.at[1, 2, s, slot]], 2)
            yield
            yield from stage(
                minor, lambda k, h: out.at[:, h, base + hi * 4 + (lo + k) % 4],
                lambda w, k: r2.at[b, w, k], (s2_s.at[b], s2_r.at[b]), 4,
            )
            yield
            tile = pl.ds(base + hi * 4 + lo, 1)

            def plane(k, h):
                s, slot = {(2, 0): (0, 0), (2, 1): (0, 1), (1, 1): (1, 0), (3, 0): (1, 1), (1, 0): (2, 0),
                           (3, 1): (2, 1), (0, 0): (3, 0), (0, 1): (3, 1)}[(k, h)]
                return out.at[s, slot, tile]

            yield from stage(
                "x", plane, lambda w, k: r3.at[b, w, k], (s3_s.at[b], s3_r.at[b]), 1,
            )
        tile = pl.ds(base + hi * 4 + lo, 1)
        final = out.at[3, :, tile]
        keep = pltpu.make_async_copy(final, spread.at[mine, tile], st_s.at[b])
        keep.start()
        yield
        yield from gather(
            minor, lambda k: pl.ds(base + hi * 4 + (lo + k) % 4, 1), final, (ag_s.at[b, 0], ag_r.at[b, 0])
        )
        keep.wait()
        yield
        group = pl.ds(base + hi * 4, 4)
        yield from gather(
            major, lambda k: pl.ds(base + ((hi + k) % 4) * 4, 4), spread.at[mine, group],
            (ag_s.at[b, 1], ag_r.at[b, 1]),
        )
        core_copy(b).start()

    def core_copy(b):
        rows = spread.at[mine, pl.ds(16 * b, 16)]
        return remote(rows, rows, co_s.at[b], co_r.at[b], partner)

    chains = [batch(b) for b in (2, 3, 0, 1)]
    while chains:
        for chain in list(chains):
            try:
                next(chain)
            except StopIteration:
                chains.remove(chain)
    for b in range(4):
        core_copy(b).wait_recv()

    def wait_exchange(i, _):
        exchange(i).wait_send()
        return 0

    lax.fori_loop(0, NC, wait_exchange, 0)
    for b in range(2):
        for way in (0, 1):
            for kind in range(3):
                put_x(b, way, kind).wait_send()

    def wait1(s, _):
        for axis in "yz":
            for way in (0, 1):
                for kind in range(3):
                    put1(axis, s, way, kind).wait_send()
        return 0

    lax.fori_loop(0, 4, wait1, 0)
    for b in range(4):
        for way in (0, 1):
            for kind in range(3):
                remote(r2.at[b, way, kind], r2.at[b, way, kind], s2_s.at[b, way, kind], s2_r.at[b, way, kind],
                       partner).wait_send()
                remote(r3.at[b, way, kind], r3.at[b, way, kind], s3_s.at[b, way, kind], s3_r.at[b, way, kind],
                       partner).wait_send()
        for stage_no, n in ((0, 1), (1, 4)):
            for i in range(4):
                part = spread.at[pl.ds(0, 2), pl.ds(0, n)] if i < 2 else spread.at[0, pl.ds(0, n)]
                remote(part, part, ag_s.at[b, stage_no, i], ag_r.at[b, stage_no, i], partner).wait_send()
        core_copy(b).wait_send()


def ladders(first, second, amp, factors):
    dma = pltpu.SemaphoreType.DMA
    any_space = pl.BlockSpec(memory_space=pl.ANY)
    smem = pl.BlockSpec(memory_space=pltpu.SMEM)
    vmem = pl.BlockSpec(memory_space=pltpu.VMEM)
    flops = 2 * FILLED * 8 * VT * VT * KC
    spread, _ = pl.pallas_call(
        ladder_kernel,
        out_shape=(
            jax.ShapeDtypeStruct((4, FILLED, VT, VT), BF),
            jax.ShapeDtypeStruct(factors.shape, BF),
        ),
        in_specs=[smem, smem, vmem, any_space],
        out_specs=(any_space, any_space),
        scratch_shapes=[
            pltpu.VMEM((4, 512, 256), BF),
            pltpu.VMEM((53, 256, 256), BF),
            pltpu.VMEM((NC, VT, KC), BF),
            pltpu.VMEM((NC, KC, 256), BF),
            pltpu.VMEM((4, 2, FILLED, VT, VT), BF),
            pltpu.VMEM((2, 2, ROWS, W * VT), BF),
            pltpu.VMEM((2, 2, 3, 16, VT, VT), BF),
            pltpu.VMEM((2, 3, 4, 2, 2, VT, VT), BF),
            pltpu.VMEM((2, 3, 4, 2, 2, VT, VT), BF),
            pltpu.VMEM((4, 2, 3, 4, VT, VT), BF),
            pltpu.VMEM((4, 2, 3, 1, VT, VT), BF),
            dma((NC,)), dma((NC,)), dma((2, 2)),
            dma((2, 2, 3)), dma((2, 2, 3)),
            dma((4, 2, 3)), dma((4, 2, 3)), dma((4, 2, 3)), dma((4, 2, 3)),
            dma((4, 2, 3)), dma((4, 2, 3)), dma((4, 2, 3)), dma((4, 2, 3)),
            dma((4, 2, 4)), dma((4, 2, 4)), dma((4,)), dma((4,)), dma((4,)),
        ],
        compiler_params=pltpu.CompilerParams(
            collective_id=0, has_side_effects=True, vmem_limit_bytes=63 * 2**20
        ),
        cost_estimate=pl.CostEstimate(flops=flops, bytes_accessed=2**24, transcendentals=0),
    )(first, second, amp, factors)
    return spread


def home_kernel(source, kept, tiles, owned, residual, out, norms, wide):
    s = pl.program_id(0)
    for p in range(4):
        wide[p * 128:p * 128 + 128, :] = tiles[p, 0].astype(F32)
    keep = kept[s] == 1
    for a in range(VT):
        lanes = slice(a * 128, a * 128 + 128)
        ladder = wide[pl.ds(a, 4, stride=128), :]
        total = residual[0, :, lanes].astype(F32) + ladder
        out[0, :, lanes] = jnp.where(keep, total, 0.0).astype(BF)

    @pl.when(s % 4 == 0)
    def _():
        for p in range(4):
            value = owned[p, 0].astype(F32)
            mean = jnp.sum(value * value) * (1.0 / (VT * VT))
            norms[s // 4, p] = mean


def at_home(source, kept, spread, residual):
    wide_index = lax.axis_index("wide")
    owner = jnp.stack([wide_index * 2, wide_index * 2 + 1]).astype(jnp.int32)

    def kernel(source_ref, kept_ref, owner_ref, *refs):
        home_kernel(source_ref, kept_ref, *refs)

    return pl.pallas_call(
        kernel,
        out_shape=(
            jax.ShapeDtypeStruct(residual.shape, BF),
            jax.ShapeDtypeStruct((2, 4), F32),
        ),
        grid_spec=pltpu.PrefetchScalarGridSpec(
            num_scalar_prefetch=3,
            grid=(8,),
            in_specs=[
                pl.BlockSpec((4, 1, VT, VT), lambda s, src, kept, own: (0, src[s], 0, 0)),
                pl.BlockSpec((4, 1, VT, VT), lambda s, src, kept, own: (0, own[s // 4], 0, 0)),
                pl.BlockSpec((1, 4, VT * VT), lambda s, src, kept, own: (s, 0, 0)),
            ],
            out_specs=[
                pl.BlockSpec((1, 4, VT * VT), lambda s, src, kept, own: (s, 0, 0)),
                pl.BlockSpec(memory_space=pltpu.SMEM),
            ],
            scratch_shapes=[pltpu.VMEM((4 * VT, VT), F32)],
        ),
    )(source, kept, owner, spread, spread, residual)


def body(factors, t2_window, residual_in, tile_mask, owner_slot, home_slot):
    tile_ids = jnp.arange(tile_mask.shape[0], dtype=jnp.int32)
    is_filled = tile_mask == 1
    owner_match = is_filled[:, None] & (owner_slot[:, None] == jnp.arange(FILLED, dtype=jnp.int32)[None, :])
    tile_of_slot = jnp.sum(jnp.where(owner_match, tile_ids[:, None], 0), axis=0).astype(jnp.int32)
    home_ids = lax.axis_index("wide") * 8 + jnp.arange(8, dtype=jnp.int32)
    present = is_filled[:, None] & (home_slot[:, None] == home_ids[None, :])
    kept = jnp.any(present, axis=0).astype(jnp.int32)
    source = jnp.sum(jnp.where(present, owner_slot[:, None], 0), axis=0).astype(jnp.int32)
    x = lax.axis_index("narrow")
    core = lax.axis_index("wide") % 2

    def pair(offset, slot):
        return ((x + offset) % 4) * 4 + core * 2 + slot

    pairs = jnp.stack([
        pair(2, 0), pair(2, 1), pair(1, 1), pair(3, 0), pair(1, 0), pair(3, 1), pair(0, 0), pair(0, 1),
    ])
    amp = jnp.take(jnp.pad(t2_window, ((0, 0), (0, 1), (0, 1))), pairs, axis=0)
    spread = ladders(tile_of_slot // NC, tile_of_slot % NC, amp, factors)
    return at_home(source, kept, spread, residual_in)


def solution(mesh):
    in_specs = (P(None, ("wide", "narrow"), None), P(), P("wide", "narrow", None), P(), P(), P())
    out_specs = (P("wide", "narrow", None), P("wide", "narrow"))
    return jax.shard_map(body, mesh=mesh, in_specs=in_specs, out_specs=out_specs, check_vma=False)
```

```python
import functools

import jax
import jax.numpy as jnp
from jax import lax
from jax.experimental import pallas as pl
from jax.experimental.pallas import tpu as pltpu
from jax.sharding import PartitionSpec as P

BF = jnp.bfloat16
F32 = jnp.float32
MESH = pl.DeviceIdType.MESH
VT = 128
W = 15
NC = 15
ROWS = 56
KC = 1792
FILLED = 64
START2, START0, START1 = 0, 2, 4


def place():
    w = lax.axis_index("wide")
    return lax.axis_index("narrow"), (w // 2) % 4, w // 8, w % 2


def at(x, y, z, c):
    return {"wide": z * 8 + y * 2 + c, "narrow": x}


def ladder_kernel(
    first, second, choice, amp, own_rows,
    spread, norms, other_rows,
    weights, f2, f1t, y_buf, out, raw, rx, ry, rz, r2, r3, done_0, done_1, done_2, done_3, squares,
    ex_s, ex_r, ld_s, x_s, x_r, y_s, y_r, z_s, z_r, s2_s, s2_r, s3_s, s3_r,
    ag_s, ag_r, aa_s, aa_r, co_s, co_r, st_s, nz_s, nz_r, ny_s, ny_r, nc_s, nc_r, nl_s,
):
    x, y, z, c = place()
    done = (done_0, done_1, done_2, done_3)
    ring = {
        "x": (x, [at((x + k) % 4, y, z, c) for k in range(4)]),
        "y": (y, [at(x, (y + k) % 4, z, c) for k in range(4)]),
        "z": (z, [at(x, y, (z + k) % 4, c) for k in range(4)]),
    }
    partner = at(x, y, z, 1 - c)

    barrier = pltpu.get_barrier_semaphore()
    greeted = [partner] + [ring[a][1][k] for a in "xyz" for k in (1, 2, 3)]
    for device in greeted:
        pl.semaphore_signal(barrier, inc=1, device_id=device, device_id_type=MESH)
    pl.semaphore_wait(barrier, len(greeted))

    def remote(src, dst, s_sem, r_sem, device):
        return pltpu.make_async_remote_copy(
            src_ref=src, dst_ref=dst, send_sem=s_sem, recv_sem=r_sem, device_id=device, device_id_type=MESH
        )

    def exchange(i):
        return remote(own_rows.at[i], other_rows.at[i], ex_s.at[i], ex_r.at[i], partner)

    def start_exchange(i, _):
        exchange(i).start()
        return 0

    lax.fori_loop(0, NC, start_exchange, 0)

    row = lax.broadcasted_iota(jnp.int32, (256, 16), 0)
    col = lax.broadcasted_iota(jnp.int32, (256, 16), 1)
    widen = (row // 16 == col).astype(F32).astype(BF)
    row2 = lax.broadcasted_iota(jnp.int32, (256, 256), 0)
    col2 = lax.broadcasted_iota(jnp.int32, (256, 256), 1)
    same = row2 % 16 == col2 % 16
    for i in range(8):
        tall = jnp.dot(widen, amp[i], preferred_element_type=F32).astype(BF)
        full = lax.dot_general(tall, widen, (((1,), (1,)), ((), ())), preferred_element_type=F32)
        weights[i // 2, (i % 2) * 256:(i % 2) * 256 + 256, :] = jnp.where(same, full, 0.0).astype(BF)

    def load(which, i):
        src = (own_rows, other_rows)[which]
        return pltpu.make_async_copy(src.at[i], raw.at[which, i % 2], ld_s.at[which, i % 2])

    def start_load(i):
        load(0, i).start()
        exchange(i).wait_recv()
        load(1, i).start()

    start_load(0)
    f2[52, :, 128:256] = jnp.zeros((256, 128), BF)

    def assemble(i, _):
        @pl.when(i + 1 < NC)
        def _():
            start_load(i + 1)

        load(0, i).wait()
        load(1, i).wait()
        slot = i % 2
        for blk in range(7):
            parts = []
            for d in range(W):
                lanes = slice(d * 128, d * 128 + 128)
                if blk < 6:
                    r0 = (blk % 3) * 16
                    parts.append(raw[blk // 3, slot, r0:r0 + 16, lanes])
                else:
                    parts.append(
                        jnp.concatenate([raw[0, slot, 48:56, lanes], raw[1, slot, 48:56, lanes]], axis=0)
                    )
            parts.append(jnp.zeros((16, 128), BF))
            block = jnp.concatenate(parts, axis=0)
            f1t[i, :, blk * 256:blk * 256 + 256] = block.T
            if blk < 6:
                f2[i * 3 + blk // 2, :, (blk % 2) * 128:(blk % 2) * 128 + 128] = block
            else:
                f2[45 + i // 2, :, pl.ds(pl.multiple_of((i % 2) * 128, 128), 128)] = block
        return 0

    lax.fori_loop(0, NC, assemble, 0)

    def put(axis, view, recv, s_sem, r_sem, way, kind):
        step = 2 if kind == 0 else (1 if way == 0 else 3)
        half = {0: way, 1: 1 - way, 2: way}[kind]
        return remote(view(step, half), recv(way, kind), s_sem(way, kind), r_sem(way, kind), ring[axis][1][3 if way else 1])

    def add_tiles(dst, terms, n, own=None):
        own = dst if own is None else own

        def one(i, _):
            total = own.at[i][...].astype(F32)
            for term in terms:
                total = total + term.at[i][...].astype(F32)
            dst.at[i][...] = total.astype(BF)
            return 0

        lax.fori_loop(0, n, one, 0)

    def view1(axis, s):
        coord, base = ring[axis][0], 32 if axis == "y" else 48
        return lambda k, h: out.at[s, :, pl.ds(base + ((coord + k) % 4) * 4 + 2 * h, 2)]

    def put1(axis, s, way, kind):
        buf, ss, rs = (ry, y_s, y_r) if axis == "y" else (rz, z_s, z_r)
        return put(
            axis, view1(axis, s), lambda w, k: buf.at[w, k, s], lambda w, k: ss.at[s, w, k],
            lambda w, k: rs.at[s, w, k], way, kind,
        )

    def later1(axis, s):
        buf = ry if axis == "y" else rz
        for way in (0, 1):
            put1(axis, s, way, 0).wait_recv()
            dst = view1(axis, s)(1 if way == 0 else 3, way)
            for slot in range(2):
                add_tiles(dst.at[slot], [buf.at[way, 0, s, slot]], 2)
            put1(axis, s, way, 2).start()

    X_AT = {(0, 0): (0, 0), (1, 0): (0, 1), (0, 1): (1, 0), (1, 1): (1, 1), (0, 2): (2, 0), (1, 2): (2, 1)}

    def put_x(b, way, kind):
        s, slot = X_AT[(way, kind)]
        return remote(
            out.at[s, slot, b * 16:b * 16 + 16], rx.at[b, way, kind], x_s.at[b, way, kind], x_r.at[b, way, kind],
            ring["x"][1][3 if way else 1],
        )

    def compute(s, b):
        def group(i, _):
            for u in range(8):
                t = b * 16 + i * 8 + u
                o = jnp.dot(f1t[first[t]], y_buf[second[t]], preferred_element_type=F32).astype(BF)
                out[s, 0, t] = o[:, :128]
                out[s, 1, t] = o[:, 128:]
            return 0

        lax.fori_loop(0, 2, group, 0)

    def amplitudes(s):
        def put_block(o, i, blk, half):
            rows = slice(blk * 256, blk * 256 + 256)
            for slot in range(2):
                y_buf[i, rows, slot * 128:slot * 128 + 128] = o[slot * 256:slot * 256 + 256, half * 128:half * 128 + 128]

        def cluster(i, _):
            for j in range(3):
                o = jnp.dot(weights[s], f2[i * 3 + j], preferred_element_type=F32).astype(BF)
                for half in range(2):
                    put_block(o, i, 2 * j + half, half)
            return 0

        lax.fori_loop(0, NC, cluster, 0)

        def tail(i, _):
            o = jnp.dot(weights[s], f2[45 + i], preferred_element_type=F32).astype(BF)
            for half in range(2):
                put_block(o, 2 * i + half, 6, half)
            return 0

        lax.fori_loop(0, 7, tail, 0)
        o = jnp.dot(weights[s], f2[52], preferred_element_type=F32).astype(BF)
        put_block(o, 14, 6, 0)

    MAJOR = ("y", "z", "y", "z")
    MINOR = ("z", "y", "z", "y")

    def corner(b):
        return 16 * b, ring[MAJOR[b]][0], ring[MINOR[b]][0]

    def put2(b, s, way, kind):
        base, hi, lo = corner(b)
        return put(
            MINOR[b], lambda k, h: out.at[s, h, base + hi * 4 + (lo + k) % 4], lambda w, k: r2.at[b, w, k, s],
            lambda w, k: s2_s.at[b, s, w, k], lambda w, k: s2_r.at[b, s, w, k], way, kind,
        )

    def send1(b, s):
        for kind in (0, 1):
            for way in (0, 1):
                put1(MAJOR[b], s, way, kind).start()

    def sum1(b, s):
        base, hi, lo = corner(b)
        buf = ry if b == 2 else rz
        for way in (0, 1):
            for kind in (1, 2):
                put1(MAJOR[b], s, way, kind).wait_recv()
        for slot in range(2):
            for half in range(2):
                own = out.at[s, slot, pl.ds(base + hi * 4 + 2 * half, 2)]
                add_tiles(own, [buf.at[half, 2, s, slot], buf.at[1 - half, 1, s, slot]], 2)
        for kind in (0, 1):
            for way in (0, 1):
                put2(b, s, way, kind).start()

    def later2(b, s):
        base, hi, lo = corner(b)
        for way in (0, 1):
            put2(b, s, way, 0).wait_recv()
            dst = out.at[s, way, base + hi * 4 + (lo + (3 if way else 1)) % 4]
            dst[...] = (dst[...].astype(F32) + r2[b, way, 0, s].astype(F32)).astype(BF)
            put2(b, s, way, 2).start()

    def sum2(b, s):
        base, hi, lo = corner(b)
        for way in (0, 1):
            for kind in (1, 2):
                put2(b, s, way, kind).wait_recv()
        for h in range(2):
            dst = out.at[s, h, base + hi * 4 + lo]
            total = dst[...].astype(F32) + r2[b, h, 2, s].astype(F32) + r2[b, 1 - h, 1, s].astype(F32)
            dst[...] = total.astype(BF)

    ACTS = (send1, lambda b, s: later1(MAJOR[b], s), sum1, later2, sum2)

    def step(s, _):
        amplitudes(s)
        for b in (0, 1):
            compute(s, b)

            @pl.when(s == 0)
            def _():
                for way in (0, 1):
                    put_x(b, way, 0).start()

            @pl.when(s == 1)
            def _():
                for way in (0, 1):
                    put_x(b, way, 1).start()

            @pl.when(s == 2)
            def _():
                for way in (0, 1):
                    put_x(b, way, 0).wait_recv()
                    add_tiles(out.at[2, way, b * 16:b * 16 + 16], [rx.at[b, way, 0]], 16)
                    put_x(b, way, 2).start()

        for b in (2, 3):
            compute(s, b)
            ACTS[0](b, s)
            for n in (1, 2, 3):
                @pl.when(s >= n)
                def _():
                    ACTS[n](b, s - n)
        return 0

    lax.fori_loop(0, 4, step, 0)

    def put2x(b, way, kind):
        base, hi, lo = corner(b)
        return put(
            MAJOR[b], lambda k, h: out.at[3, h, pl.ds(base + ((hi + k) % 4) * 4, 4)], lambda w, k: r2.at[b, w, k],
            lambda w, k: s2_s.at[b, 0, w, k], lambda w, k: s2_r.at[b, 0, w, k], way, kind,
        )

    PLANES = {1: ((2, 0), (1, 0)), 2: ((0, 0), (0, 1)), 3: ((1, 1), (2, 1))}

    def put3(b, k, h):
        base, hi, lo = corner(b)
        if b < 2:
            src, axis = out.at[3, h, base + hi * 4 + (lo + k) % 4], MINOR[b]
        else:
            s, slot = PLANES[k][h]
            src, axis = out.at[s, slot, base + hi * 4 + lo], "x"
        return remote(src, r3.at[b, k - 1, h], s3_s.at[b, k - 1, h], s3_r.at[b, k - 1, h], ring[axis][1][k])

    def share(b, k):
        base, hi, lo = corner(b)
        return remote(done[b].at[lo], done[b].at[lo], ag_s.at[b, k - 1], ag_r.at[b, k - 1], ring[MINOR[b]][1][k])

    def packed(b, k):
        return rx.at[b // 2, b % 2, 0, 2 * k:2 * k + 2]

    def deliver(b, k):
        base, hi, lo = corner(b)
        cell = spread.at[c, 4 * b + hi]
        if k == 0:
            return pltpu.make_async_copy(packed(b, 0), cell, st_s.at[b])
        return remote(packed(b, k), cell, aa_s.at[b, k - 1], aa_r.at[b, k - 1], ring[MAJOR[b]][1][k])

    def core_copy(b):
        rows = spread.at[c, 4 * b:4 * b + 4]
        return remote(rows, rows, co_s.at[b], co_r.at[b], partner)

    def batch(b):
        base, hi, lo = corner(b)
        if b < 2:
            for way in (0, 1):
                for kind in (1, 2):
                    put_x(b, way, kind).wait_recv()
            for half in range(2):
                add_tiles(out.at[3, half, base:base + 16], [rx.at[b, half, 2], rx.at[b, 1 - half, 1]], 16)
            for kind in (0, 1):
                for way in (0, 1):
                    put2x(b, way, kind).start()
            yield
            for way in (0, 1):
                put2x(b, way, 0).wait_recv()
                near = pl.ds(base + ((hi + (3 if way else 1)) % 4) * 4, 4)
                add_tiles(out.at[3, way, near], [r2.at[b, way, 0]], 4)
                put2x(b, way, 2).start()
            yield
            for way in (0, 1):
                for kind in (1, 2):
                    put2x(b, way, kind).wait_recv()
            for half in range(2):
                add_tiles(out.at[3, half, pl.ds(base + hi * 4, 4)], [r2.at[b, half, 2], r2.at[b, 1 - half, 1]], 4)
        else:
            for turn in range(4):
                for n in (1, 2, 3, 4):
                    s = turn + 4 - n
                    if s < 4:
                        ACTS[n](b, s)
                if turn < 3:
                    yield
        for k in (2, 1, 3):
            for h in range(2):
                put3(b, k, h).start()
        yield
        for k in (1, 2, 3):
            for h in range(2):
                put3(b, k, h).wait_recv()
        for h in range(2):
            total = out[3, h, base + hi * 4 + lo].astype(F32)
            for k in range(3):
                total = total + r3[b, k, h].astype(F32)
            tile = total.astype(BF)
            done[b][lo, h] = tile
            value = tile.astype(F32)
            mean = jnp.sum(value * value, keepdims=True) * (1.0 / (VT * VT))
            squares[c, z, y, 2 * b + h:2 * b + h + 1, :] = jnp.broadcast_to(mean, (1, 128))
        for k in (2, 1, 3):
            share(b, k).start()
        yield
        for k in (1, 2, 3):
            share(b, k).wait_recv()
        for k in (2, 1, 3, 0):
            for h in range(2):
                rx[b // 2, b % 2, 0, 2 * k + h] = done[b][choice[4 * b + k], h]
            deliver(b, k).start()
        yield
        deliver(b, 0).wait()
        for k in (1, 2, 3):
            deliver(b, k).wait_recv()
        core_copy(b).start()

    def norms_z(k):
        part = squares.at[c, z, y]
        return remote(part, part, nz_s.at[k - 1], nz_r.at[k - 1], ring["z"][1][k])

    def norms_y(k):
        part = squares.at[c, :, y]
        return remote(part, part, ny_s.at[k - 1], ny_r.at[k - 1], ring["y"][1][k])

    def norms_core():
        return remote(squares.at[c], norms.at[c], nc_s, nc_r, partner)

    def all_norms():
        for k in (1, 2, 3):
            norms_z(k).start()
        yield
        for k in (1, 2, 3):
            norms_z(k).wait_recv()
        for k in (1, 2, 3):
            norms_y(k).start()
        yield
        for k in (1, 2, 3):
            norms_y(k).wait_recv()
        norms_core().start()
        keep = pltpu.make_async_copy(squares.at[c], norms.at[c], nl_s)
        keep.start()
        yield
        keep.wait()
        norms_core().wait_recv()

    order = [(START2, batch(2)), (START2, batch(3)), (START0, batch(0)), (START1, batch(1))]
    waiting = list(order)
    running = []
    turn = 0
    ready = False
    while waiting or running:
        running += [chain for when, chain in waiting if when <= turn]
        waiting = [(when, chain) for when, chain in waiting if when > turn]
        for chain in list(running):
            try:
                next(chain)
            except StopIteration:
                running.remove(chain)
        turn += 1
        if not ready and turn == START1 + 4:
            running.append(all_norms())
            ready = True
    for b in range(4):
        core_copy(b).wait_recv()

    def wait_exchange(i, _):
        exchange(i).wait_send()
        return 0

    lax.fori_loop(0, NC, wait_exchange, 0)

    def wait_steps(s, _):
        for way in (0, 1):
            for kind in range(3):
                for axis in "yz":
                    put1(axis, s, way, kind).wait_send()
                for b in (2, 3):
                    put2(b, s, way, kind).wait_send()
        return 0

    lax.fori_loop(0, 4, wait_steps, 0)
    for b in range(4):
        for way in (0, 1):
            for kind in range(3):
                if b < 2:
                    put_x(b, way, kind).wait_send()
                    put2x(b, way, kind).wait_send()
        for k in (1, 2, 3):
            for h in range(2):
                put3(b, k, h).wait_send()
            share(b, k).wait_send()
            deliver(b, k).wait_send()
        core_copy(b).wait_send()
    for k in (1, 2, 3):
        norms_z(k).wait_send()
        norms_y(k).wait_send()
    norms_core().wait_send()


def ladders(first, second, choice, amp, factors):
    dma = pltpu.SemaphoreType.DMA
    any_space = pl.BlockSpec(memory_space=pl.ANY)
    smem = pl.BlockSpec(memory_space=pltpu.SMEM)
    vmem = pl.BlockSpec(memory_space=pltpu.VMEM)
    flops = 2 * FILLED * 8 * VT * VT * KC
    spread, norms, _ = pl.pallas_call(
        ladder_kernel,
        out_shape=(
            jax.ShapeDtypeStruct((2, 16, 2, VT, VT), BF),
            jax.ShapeDtypeStruct((2, 4, 4, 8, 128), F32),
            jax.ShapeDtypeStruct(factors.shape, BF),
        ),
        in_specs=[smem, smem, smem, vmem, any_space],
        out_specs=(any_space, any_space, any_space),
        scratch_shapes=[
            pltpu.VMEM((4, 512, 256), BF),
            pltpu.VMEM((53, 256, 256), BF),
            pltpu.VMEM((NC, VT, KC), BF),
            pltpu.VMEM((NC, KC, 256), BF),
            pltpu.VMEM((4, 2, FILLED, VT, VT), BF),
            pltpu.VMEM((2, 2, ROWS, W * VT), BF),
            pltpu.VMEM((2, 2, 3, 16, VT, VT), BF),
            pltpu.VMEM((2, 3, 4, 2, 2, VT, VT), BF),
            pltpu.VMEM((2, 3, 4, 2, 2, VT, VT), BF),
            pltpu.VMEM((4, 2, 3, 4, VT, VT), BF),
            pltpu.VMEM((4, 3, 2, VT, VT), BF),
            pltpu.VMEM((4, 2, VT, VT), BF),
            pltpu.VMEM((4, 2, VT, VT), BF),
            pltpu.VMEM((4, 2, VT, VT), BF),
            pltpu.VMEM((4, 2, VT, VT), BF),
            pltpu.VMEM((2, 4, 4, 8, 128), F32),
            dma((NC,)), dma((NC,)), dma((2, 2)),
            dma((2, 2, 3)), dma((2, 2, 3)),
            dma((4, 2, 3)), dma((4, 2, 3)), dma((4, 2, 3)), dma((4, 2, 3)),
            dma((4, 4, 2, 3)), dma((4, 4, 2, 3)), dma((4, 3, 2)), dma((4, 3, 2)),
            dma((4, 3)), dma((4, 3)), dma((4, 3)), dma((4, 3)),
            dma((4,)), dma((4,)), dma((4,)),
            dma((3,)), dma((3,)), dma((3,)), dma((3,)), dma, dma, dma,
        ],
        compiler_params=pltpu.CompilerParams(
            collective_id=0, has_side_effects=True, vmem_limit_bytes=63 * 2**20
        ),
        cost_estimate=pl.CostEstimate(flops=flops, bytes_accessed=2**24, transcendentals=0),
    )(first, second, choice, amp, factors)
    return spread, norms


def home_kernel(source, kept, norm_row, tiles, norms, residual, out, norms_out, wide):
    s = pl.program_id(0)
    for p in range(4):
        wide[p * 128:p * 128 + 128, :] = tiles[p // 2, 0, p % 2].astype(F32)
    keep = kept[s] == 1
    for a in range(VT):
        lanes = slice(a * 128, a * 128 + 128)
        ladder = wide[pl.ds(a, 4, stride=128), :]
        total = residual[0, :, lanes].astype(F32) + ladder
        out[0, :, lanes] = jnp.where(keep, total, 0.0).astype(BF)

    @pl.when(s == 0)
    def _():
        for i in range(2):
            for p in range(4):
                row = norms[pl.ds((p // 2) * 128 + norm_row[i] + p % 2, 1), :]
                norms_out[i, p] = jnp.max(row)


def at_home(source, kept, norm_row, spread, norms, residual):
    return pl.pallas_call(
        home_kernel,
        out_shape=(
            jax.ShapeDtypeStruct(residual.shape, BF),
            jax.ShapeDtypeStruct((2, 4), F32),
        ),
        grid_spec=pltpu.PrefetchScalarGridSpec(
            num_scalar_prefetch=3,
            grid=(8,),
            in_specs=[
                pl.BlockSpec((2, 1, 2, VT, VT), lambda s, src, kept, row: (0, src[s], 0, 0, 0)),
                pl.BlockSpec((256, 128), lambda s, src, kept, row: (0, 0)),
                pl.BlockSpec((1, 4, VT * VT), lambda s, src, kept, row: (s, 0, 0)),
            ],
            out_specs=[
                pl.BlockSpec((1, 4, VT * VT), lambda s, src, kept, row: (s, 0, 0)),
                pl.BlockSpec(memory_space=pltpu.SMEM),
            ],
            scratch_shapes=[pltpu.VMEM((4 * VT, VT), F32)],
        ),
    )(source, kept, norm_row, spread, norms.reshape(256, 128), residual)


def body(factors, t2_window, residual_in, tile_mask, owner_slot, home_slot):
    x = lax.axis_index("narrow")
    wide_index = lax.axis_index("wide")
    core, own_y, own_z = wide_index % 2, (wide_index // 2) % 4, wide_index // 8
    filled = tile_mask == 1
    ids = jnp.arange(tile_mask.shape[0], dtype=jnp.int32)
    before = filled[None, :] & (home_slot[None, :] < home_slot[:, None])
    place_of = jnp.sum(before.astype(jnp.int32), axis=1)
    index_of = (place_of % 16) * 4 + place_of // 16
    match = filled[:, None] & (index_of[:, None] == jnp.arange(FILLED, dtype=jnp.int32)[None, :])
    tile_at = jnp.sum(jnp.where(match, ids[:, None], 0), axis=0).astype(jnp.int32)
    chip_at = (jnp.sum(jnp.where(match, home_slot[:, None], 0), axis=0) // 16).reshape(4, 4, 4)
    by_y = jnp.arange(4, dtype=jnp.int32) % 2 == 0
    group = jnp.where(by_y, own_y, own_z)
    cell_chips = jnp.sum(
        jnp.where(jnp.arange(4, dtype=jnp.int32)[None, :, None] == group[:, None, None], chip_at, 0), axis=1
    )
    far = (group[:, None] + jnp.arange(4, dtype=jnp.int32)[None, :]) % 4
    target = jnp.where(by_y[:, None], own_z * 4 + far, far * 4 + own_y)
    choice = jnp.sum(
        jnp.where(cell_chips[:, None, :] == target[:, :, None], jnp.arange(4, dtype=jnp.int32)[None, None, :], 0),
        axis=2,
    ).astype(jnp.int32).reshape(16)
    home_ids = wide_index * 8 + jnp.arange(8, dtype=jnp.int32)
    present = filled[:, None] & (home_slot[:, None] == home_ids[None, :])
    kept = jnp.any(present, axis=0).astype(jnp.int32)
    source = jnp.sum(jnp.where(present, index_of[:, None] // 4, 0), axis=0).astype(jnp.int32)
    owner_ids = wide_index * 2 + jnp.arange(2, dtype=jnp.int32)
    owned = filled[:, None] & (owner_slot[:, None] == owner_ids[None, :])
    batch, grp, turn = index_of // 16, (index_of // 4) % 4, index_of % 4
    row_of = jnp.where(batch % 2 == 0, turn * 4 + grp, grp * 4 + turn) * 8 + 2 * batch
    norm_row = jnp.sum(jnp.where(owned, row_of[:, None], 0), axis=0).astype(jnp.int32)

    def pair(offset, slot):
        return ((x + offset) % 4) * 4 + core * 2 + slot

    pairs = jnp.stack([
        pair(2, 0), pair(2, 1), pair(1, 1), pair(3, 0), pair(1, 0), pair(3, 1), pair(0, 0), pair(0, 1),
    ])
    amp = jnp.take(jnp.pad(t2_window, ((0, 0), (0, 1), (0, 1))), pairs, axis=0)
    spread, norms = ladders(tile_at // NC, tile_at % NC, choice, amp, factors)
    return at_home(source, kept, norm_row, spread, norms, residual_in)


def solution(mesh):
    in_specs = (P(None, ("wide", "narrow"), None), P(), P("wide", "narrow", None), P(), P(), P())
    out_specs = (P("wide", "narrow", None), P("wide", "narrow"))
    return jax.shard_map(body, mesh=mesh, in_specs=in_specs, out_specs=out_specs, check_vma=False)
```

```python
import functools

import jax
import jax.numpy as jnp
from jax import lax
from jax.experimental import pallas as pl
from jax.experimental.pallas import tpu as pltpu
from jax.sharding import PartitionSpec as P

BF = jnp.bfloat16
F32 = jnp.float32
I32 = jnp.int32
MESH = pl.DeviceIdType.MESH
VT = 128
W = 15
NC = 15
NT = 225
ROWS = 56
KC = 1792
FILLED = 64
MAJOR = ("y", "z", "y", "z")
MINOR = ("z", "y", "z", "y")
UNITS = [(b, p) for p in (0, 1) for b in range(4)]
X_FIRST = {(0, 0), (1, 0), (0, 1), (1, 1)}


X_WHEN = {
    (0, 0): (0, 4, 11, 12, 13),
    (1, 0): (1, 5, 12, 13, 14),
    (0, 1): (8, 12, 17, 18, 19),
    (1, 1): (9, 13, 17, 18, 19),
}
M_GAP = 2
REST_GAP = 1


def place():
    w = lax.axis_index("wide")
    return lax.axis_index("narrow"), (w // 2) % 4, w // 8, w % 2


def at(x, y, z, c):
    return {"wide": z * 8 + y * 2 + c, "narrow": x}


def ladder_kernel(plan, t2, own_rows, spread, norms, other_rows, *scratch):
    weights, f2, f1t, y_buf, out, raw, r1, r2, r3 = scratch[:9]
    done = dict(zip(UNITS, scratch[9:17]))
    (squares, ex_s, ex_r, ld_s, s1_s, s1_r, s2_s, s2_r, s3_s, s3_r, ag_s, ag_r, aa_s, aa_r, co_s, co_r, st_s,
     nz_s, nz_r, ny_s, ny_r, nc_s, nc_r, nl_s) = scratch[17:]
    x, y, z, c = place()
    ring = {
        "x": (x, [at((x + k) % 4, y, z, c) for k in range(4)]),
        "y": (y, [at(x, (y + k) % 4, z, c) for k in range(4)]),
        "z": (z, [at(x, y, (z + k) % 4, c) for k in range(4)]),
    }
    partner = at(x, y, z, 1 - c)

    barrier = pltpu.get_barrier_semaphore()
    greeted = [partner] + [ring[a][1][k] for a in "xyz" for k in (1, 2, 3)]
    for device in greeted:
        pl.semaphore_signal(barrier, inc=1, device_id=device, device_id_type=MESH)
    pl.semaphore_wait(barrier, len(greeted))

    def remote(src, dst, s_sem, r_sem, device):
        return pltpu.make_async_remote_copy(
            src_ref=src, dst_ref=dst, send_sem=s_sem, recv_sem=r_sem, device_id=device, device_id_type=MESH
        )

    def exchange(i):
        return remote(own_rows.at[i], other_rows.at[i], ex_s.at[i], ex_r.at[i], partner)

    def start_exchange(i, _):
        exchange(i).start()
        return 0

    lax.fori_loop(0, NC, start_exchange, 0)

    def load(which, i):
        src = (own_rows, other_rows)[which]
        return pltpu.make_async_copy(src.at[i], raw.at[which, i % 3], ld_s.at[which, i % 3])

    load(0, 0).start()
    load(0, 1).start()

    row = lax.broadcasted_iota(I32, (256, W), 0)
    col = lax.broadcasted_iota(I32, (256, W), 1)
    widen = (row // 16 == col).astype(F32).astype(BF)
    row2 = lax.broadcasted_iota(I32, (256, 256), 0)
    col2 = lax.broadcasted_iota(I32, (256, 256), 1)
    same = row2 % 16 == col2 % 16
    for s in range(4):
        for slot in range(2):
            ahead = (2, 1, 3, 0)[(s % 2) * 2 + slot]
            pair = ((x + ahead) % 4) * 4 + c * 2 + s // 2
            tall = jnp.dot(widen, t2[pair], preferred_element_type=F32).astype(BF)
            full = lax.dot_general(tall, widen, (((1,), (1,)), ((), ())), preferred_element_type=F32)
            weights[s, slot * 256:slot * 256 + 256, :] = jnp.where(same, full, 0.0).astype(BF)
    f2[52, :, 128:256] = jnp.zeros((256, 128), BF)

    def assemble(i, blocks):
        slot = i % 3
        for blk in blocks:
            parts = []
            for d in range(W):
                lanes = slice(d * 128, d * 128 + 128)
                if blk < 6:
                    r0 = (blk % 3) * 16
                    parts.append(raw[blk // 3, slot, r0:r0 + 16, lanes])
                else:
                    parts.append(
                        jnp.concatenate([raw[0, slot, 48:56, lanes], raw[1, slot, 48:56, lanes]], axis=0)
                    )
            parts.append(jnp.zeros((16, 128), BF))
            block = jnp.concatenate(parts, axis=0)
            f1t[i, :, blk * 256:blk * 256 + 256] = block.T
            if blk < 6:
                f2[i * 3 + blk // 2, :, (blk % 2) * 128:(blk % 2) * 128 + 128] = block
            else:
                f2[45 + i // 2, :, pl.ds(pl.multiple_of((i % 2) * 128, 128), 128)] = block

    def assemble_own(i, _):
        @pl.when(i + 2 < NC)
        def _():
            load(0, i + 2).start()

        load(0, i).wait()
        assemble(i, (0, 1, 2))
        return 0

    lax.fori_loop(0, NC, assemble_own, 0)

    def put_block(o, i, blk, half):
        rows = slice(blk * 256, blk * 256 + 256)
        for slot in range(2):
            y_buf[i, rows, slot * 128:slot * 128 + 128] = o[slot * 256:slot * 256 + 256, half * 128:half * 128 + 128]

    def amplitude_pairs(s, pairs):
        def cluster(n, _):
            for u in range(3):
                for j in pairs:
                    i = n * 3 + u
                    o = jnp.dot(weights[s], f2[i * 3 + j], preferred_element_type=F32).astype(BF)
                    for half in range(2):
                        put_block(o, i, 2 * j + half, half)
            return 0

        lax.fori_loop(0, NC // 3, cluster, 0)

    def amplitude_last(s):
        for i in range(8):
            o = jnp.dot(weights[s], f2[45 + i], preferred_element_type=F32).astype(BF)
            for half in range(2):
                if 2 * i + half < NC:
                    put_block(o, 2 * i + half, 6, half)

    amplitude_pairs(0, (0,))

    def start_both(i):
        load(0, i).start()
        exchange(i).wait_recv()
        load(1, i).start()

    start_both(0)
    start_both(1)

    def assemble_other(i, _):
        @pl.when(i + 2 < NC)
        def _():
            start_both(i + 2)

        load(0, i).wait()
        load(1, i).wait()
        assemble(i, (3, 4, 5, 6))
        return 0

    lax.fori_loop(0, NC, assemble_other, 0)

    def compute(s, b):
        for i in range(16):
            t = b * 16 + i
            o = jnp.dot(f1t[plan[0, t]], y_buf[plan[1, t]], preferred_element_type=F32).astype(BF)
            out[s, 0, t] = o[:, :128]
            out[s, 1, t] = o[:, 128:]

    def add_tiles(dst, terms, n):
        def one(i, _):
            total = dst.at[i][...].astype(F32)
            for term in terms:
                total = total + term.at[i][...].astype(F32)
            dst.at[i][...] = total.astype(BF)
            return 0

        lax.fori_loop(0, n, one, 0)

    def route(way, kind):
        return (2 if kind == 0 else (3 if way else 1)), (1 - way if kind == 1 else way)

    def corner(b):
        return 16 * b, ring[MAJOR[b]][0], ring[MINOR[b]][0]

    def number(unit):
        return unit[1] * 4 + unit[0]

    PLANE = {2: (0, 0), 1: (0, 1), 3: (1, 0), 0: (1, 1)}

    def x_part(unit, k, half):
        b, p = unit
        s, slot = PLANE[k]
        return out.at[2 * p + s, slot, 16 * b + 8 * half:16 * b + 8 * half + 8]

    def x_put(unit, way, kind):
        u = number(unit)
        return remote(
            x_part(unit, *route(way, kind)), r1.at[u, way, kind], s1_s.at[u, way, kind, 0],
            s1_r.at[u, way, kind, 0], ring["x"][1][3 if way else 1],
        )

    def x_begin(unit):
        x_put(unit, 0, 0).start()
        x_put(unit, 1, 0).start()
        x_put(unit, 0, 1).start()

    def x_pass(unit):
        x_put(unit, 1, 1).start()
        for way in (0, 1):
            x_put(unit, way, 0).wait_recv()
            add_tiles(x_part(unit, *route(way, 2)), [r1.at[number(unit), way, 0]], 8)
            x_put(unit, way, 2).start()

    def x_sum(unit):
        u = number(unit)
        for way in (0, 1):
            for kind in (1, 2):
                x_put(unit, way, kind).wait_recv()
        for half in range(2):
            add_tiles(x_part(unit, 0, half), [r1.at[u, half, 2], r1.at[u, 1 - half, 1]], 8)
        for kind in (0, 1):
            for way in (0, 1):
                x2_put(unit, way, kind).start()

    def x2_part(unit, k, half):
        b, p = unit
        base, hi, lo = corner(b)
        return out.at[2 * p + 1, 1, pl.ds(base + ((hi + k) % 4) * 4 + 2 * half, 2)]

    def x2_put(unit, way, kind):
        u = number(unit)
        return remote(
            x2_part(unit, *route(way, kind)), r2.at[u, way, kind], s2_s.at[u, way, kind, 0],
            s2_r.at[u, way, kind, 0], ring[MAJOR[unit[0]]][1][3 if way else 1],
        )

    def x2_pass(unit):
        for way in (0, 1):
            x2_put(unit, way, 0).wait_recv()
            add_tiles(x2_part(unit, *route(way, 2)), [r2.at[number(unit), way, 0]], 2)
            x2_put(unit, way, 2).start()

    def x2_sum(unit):
        u = number(unit)
        for way in (0, 1):
            for kind in (1, 2):
                x2_put(unit, way, kind).wait_recv()
        for half in range(2):
            add_tiles(x2_part(unit, 0, half), [r2.at[u, half, 2], r2.at[u, 1 - half, 1]], 2)
        last_send(unit)

    def m_part(unit, s, k, half):
        b, p = unit
        base, hi, lo = corner(b)
        return out.at[2 * p + s, :, pl.ds(base + ((hi + k) % 4) * 4 + 2 * half, 2)]

    def m_land(unit, s, way, kind):
        return r1.at[number(unit), way, kind, 4 * s:4 * s + 4]

    def m_put(unit, s, slot, way, kind):
        u = number(unit)
        return remote(
            m_part(unit, s, *route(way, kind)).at[slot], m_land(unit, s, way, kind).at[2 * slot:2 * slot + 2],
            s1_s.at[u, way, kind, 2 * s + slot], s1_r.at[u, way, kind, 2 * s + slot],
            ring[MAJOR[unit[0]]][1][3 if way else 1],
        )

    def m_begin(unit, s):
        for kind in (0, 1):
            for way in (0, 1):
                for slot in range(2):
                    m_put(unit, s, slot, way, kind).start()

    def m_pass(unit, s):
        for way in (0, 1):
            for slot in range(2):
                m_put(unit, s, slot, way, 0).wait_recv()
                add_tiles(
                    m_part(unit, s, *route(way, 2)).at[slot], [m_land(unit, s, way, 0).at[2 * slot:2 * slot + 2]], 2
                )
                m_put(unit, s, slot, way, 2).start()

    def m_sum(unit, s):
        for way in (0, 1):
            for kind in (1, 2):
                for slot in range(2):
                    m_put(unit, s, slot, way, kind).wait_recv()
        for half in range(2):
            for slot in range(2):
                two = slice(2 * slot, 2 * slot + 2)
                add_tiles(
                    m_part(unit, s, 0, half).at[slot],
                    [m_land(unit, s, half, 2).at[two], m_land(unit, s, 1 - half, 1).at[two]], 2,
                )
        for kind in (0, 1):
            for way in (0, 1):
                m2_put(unit, s, way, kind).start()

    def m2_part(unit, s, k, half):
        b, p = unit
        base, hi, lo = corner(b)
        return out.at[2 * p + s, half, base + hi * 4 + (lo + k) % 4]

    def m2_put(unit, s, way, kind):
        u = number(unit)
        return remote(
            m2_part(unit, s, *route(way, kind)), r2.at[u, way, kind, s], s2_s.at[u, way, kind, s],
            s2_r.at[u, way, kind, s], ring[MINOR[unit[0]]][1][3 if way else 1],
        )

    def m2_pass(unit, s):
        for way in (0, 1):
            m2_put(unit, s, way, 0).wait_recv()
            dst = m2_part(unit, s, *route(way, 2))
            dst[...] = (dst[...].astype(F32) + r2[number(unit), way, 0, s].astype(F32)).astype(BF)
            m2_put(unit, s, way, 2).start()

    def m2_sum(unit, s):
        u = number(unit)
        for way in (0, 1):
            for kind in (1, 2):
                m2_put(unit, s, way, kind).wait_recv()
        for half in range(2):
            dst = m2_part(unit, s, 0, half)
            total = dst[...].astype(F32) + r2[u, half, 2, s].astype(F32) + r2[u, 1 - half, 1, s].astype(F32)
            dst[...] = total.astype(BF)
        if s == 1:
            last_send(unit)

    def last_part(unit, k):
        b, p = unit
        base, hi, lo = corner(b)
        if unit in X_FIRST:
            return out.at[2 * p + 1, 1, base + hi * 4 + (lo + k) % 4]
        s, slot = PLANE[k]
        return out.at[2 * p + s, slot, base + hi * 4 + lo]

    def last_put(unit, k):
        u = number(unit)
        axis = MINOR[unit[0]] if unit in X_FIRST else "x"
        return remote(last_part(unit, k), r3.at[u, k - 1], s3_s.at[u, k - 1], s3_r.at[u, k - 1], ring[axis][1][k])

    def last_send(unit):
        for k in (2, 1, 3):
            last_put(unit, k).start()

    def last_sum(unit):
        b, p = unit
        u = number(unit)
        base, hi, lo = corner(b)
        for k in (1, 2, 3):
            last_put(unit, k).wait_recv()
        total = last_part(unit, 0)[...].astype(F32)
        for k in range(3):
            total = total + r3[u, k].astype(F32)
        tile = total.astype(BF)
        done[unit][lo] = tile
        for k in (2, 1, 3):
            share(unit, k).start()
        value = tile.astype(F32)
        mean = jnp.sum(value * value, keepdims=True) * (1.0 / (VT * VT))
        squares[c, z, y, 2 * b + p:2 * b + p + 1, :] = jnp.broadcast_to(mean, (1, 128))

    def share(unit, k):
        u = number(unit)
        lo = corner(unit[0])[2]
        return remote(
            done[unit].at[lo], done[unit].at[lo], ag_s.at[u, k - 1], ag_r.at[u, k - 1], ring[MINOR[unit[0]]][1][k]
        )

    def packed(unit, k):
        return r1.at[number(unit), 0, 0, k]

    def deliver(unit, k):
        b, p = unit
        u = number(unit)
        cell = spread.at[c, p, 4 * b + corner(b)[1]]
        if k == 0:
            return pltpu.make_async_copy(packed(unit, 0), cell, st_s.at[u])
        return remote(packed(unit, k), cell, aa_s.at[u, k - 1], aa_r.at[u, k - 1], ring[MAJOR[b]][1][k])

    def handout(unit):
        b, p = unit
        for k in (1, 2, 3):
            share(unit, k).wait_recv()
        for k in (2, 1, 3, 0):
            r1[number(unit), 0, 0, k] = done[unit][plan[2, 4 * b + k]]
            deliver(unit, k).start()

    def core_copy(unit):
        b, p = unit
        rows = spread.at[c, p, 4 * b:4 * b + 4]
        return remote(rows, rows, co_s.at[number(unit)], co_r.at[number(unit)], partner)

    def finish(unit):
        deliver(unit, 0).wait()
        for k in (1, 2, 3):
            deliver(unit, k).wait_recv()
        core_copy(unit).start()

    def phases(unit):
        bind = functools.partial
        if unit in X_FIRST:
            first = [bind(f, unit) for f in (x_begin, x_pass, x_sum, x2_pass, x2_sum)]
        else:
            acts = (m_begin, m_pass, m_sum, m2_pass, m2_sum)
            first = [[bind(f, unit, s) for f in acts] for s in (0, 1)]
        return first, [bind(f, unit) for f in (last_sum, handout, finish)]

    def norms_z(k):
        part = squares.at[c, z, y]
        return remote(part, part, nz_s.at[k - 1], nz_r.at[k - 1], ring["z"][1][k])

    def norms_y(k):
        part = squares.at[c, :, y]
        return remote(part, part, ny_s.at[k - 1], ny_r.at[k - 1], ring["y"][1][k])

    def norms_core():
        return remote(squares.at[c], norms.at[c], nc_s, nc_r, partner)

    def norms_keep():
        return pltpu.make_async_copy(squares.at[c], norms.at[c], nl_s)

    def norms_begin():
        for k in (1, 2, 3):
            norms_z(k).start()

    def norms_next():
        for k in (1, 2, 3):
            norms_z(k).wait_recv()
        for k in (1, 2, 3):
            norms_y(k).start()

    def norms_last():
        for k in (1, 2, 3):
            norms_y(k).wait_recv()
        norms_core().start()
        norms_keep().start()

    events = []
    for unit in UNITS:
        b, p = unit
        first, rest = phases(unit)
        if unit in X_FIRST:
            when = X_WHEN[unit]
            last = when[-1]
            events += list(zip(when, first))
        else:
            for s in (0, 1):
                start = 8 * p + 4 * s + b
                when = [start, start + M_GAP, start + 2 * M_GAP, start + 3 * M_GAP, start + 4 * M_GAP]
                if start + M_GAP > 15:
                    when = [start] + [max(16, start) + n for n in range(4)]
                else:
                    when = [w if w <= 15 else 16 + n - [v <= 15 for v in when].count(True) for n, w in enumerate(when)]
                last = when[-1]
                events += list(zip(when, first[s]))
        for act in rest:
            last = last + REST_GAP if last + REST_GAP <= 15 else max(16, last + 1)
            events.append((last, act))
    end = max(when for when, act in events)
    norm_at = end - 1
    events += [(norm_at + n, act) for n, act in enumerate((norms_begin, norms_next, norms_last))]
    events = sorted(enumerate(events), key=lambda e: (e[1][0], e[0]))
    by_slot = {}
    for _, (when, act) in events:
        by_slot.setdefault(when, []).append(act)

    def step(s, _):
        @pl.when(s > 0)
        def _():
            amplitude_pairs(s, (0,))

        amplitude_pairs(s, (1, 2))
        amplitude_last(s)
        for b in range(4):
            compute(s, b)
            for k in range(4):
                acts = by_slot.get(4 * k + b, [])
                if acts:
                    @pl.when(s == k)
                    def _():
                        for act in acts:
                            act()
        return 0

    lax.fori_loop(0, 4, step, 0)
    for when in sorted(by_slot):
        if when > 15:
            for act in by_slot[when]:
                act()

    for unit in UNITS:
        core_copy(unit).wait_recv()
    norms_keep().wait()
    norms_core().wait_recv()

    def wait_exchange(i, _):
        exchange(i).wait_send()
        return 0

    lax.fori_loop(0, NC, wait_exchange, 0)
    for unit in UNITS:
        for way in (0, 1):
            for kind in range(3):
                if unit in X_FIRST:
                    x_put(unit, way, kind).wait_send()
                    x2_put(unit, way, kind).wait_send()
                else:
                    for s in (0, 1):
                        for slot in (0, 1):
                            m_put(unit, s, slot, way, kind).wait_send()
                        m2_put(unit, s, way, kind).wait_send()
        for k in (1, 2, 3):
            last_put(unit, k).wait_send()
            share(unit, k).wait_send()
            deliver(unit, k).wait_send()
        core_copy(unit).wait_send()
    for k in (1, 2, 3):
        norms_z(k).wait_send()
        norms_y(k).wait_send()
    norms_core().wait_send()


def ladders(plan, t2_window, factors):
    dma = pltpu.SemaphoreType.DMA
    any_space = pl.BlockSpec(memory_space=pl.ANY)
    smem = pl.BlockSpec(memory_space=pltpu.SMEM)
    vmem = pl.BlockSpec(memory_space=pltpu.VMEM)
    flops = 2 * FILLED * 8 * VT * VT * KC
    spread, norms, _ = pl.pallas_call(
        ladder_kernel,
        out_shape=(
            jax.ShapeDtypeStruct((2, 2, 16, VT, VT), BF),
            jax.ShapeDtypeStruct((2, 4, 4, 8, 128), F32),
            jax.ShapeDtypeStruct(factors.shape, BF),
        ),
        in_specs=[smem, vmem, any_space],
        out_specs=(any_space, any_space, any_space),
        scratch_shapes=[
            pltpu.VMEM((4, 512, 256), BF),
            pltpu.VMEM((53, 256, 256), BF),
            pltpu.VMEM((NC, VT, KC), BF),
            pltpu.VMEM((NC, KC, 256), BF),
            pltpu.VMEM((4, 2, FILLED, VT, VT), BF),
            pltpu.VMEM((2, 3, ROWS, W * VT), BF),
            pltpu.VMEM((8, 2, 3, 8, VT, VT), BF),
            pltpu.VMEM((8, 2, 3, 2, VT, VT), BF),
            pltpu.VMEM((8, 3, VT, VT), BF),
        ]
        + [pltpu.VMEM((4, VT, VT), BF) for _ in UNITS]
        + [
            pltpu.VMEM((2, 4, 4, 8, 128), F32),
            dma((NC,)), dma((NC,)), dma((2, 3)),
            dma((8, 2, 3, 4)), dma((8, 2, 3, 4)), dma((8, 2, 3, 2)), dma((8, 2, 3, 2)), dma((8, 3)), dma((8, 3)),
            dma((8, 3)), dma((8, 3)), dma((8, 3)), dma((8, 3)), dma((8,)), dma((8,)), dma((8,)),
            dma((3,)), dma((3,)), dma((3,)), dma((3,)), dma, dma, dma,
        ],
        compiler_params=pltpu.CompilerParams(
            collective_id=0, has_side_effects=True, vmem_limit_bytes=63 * 2**20
        ),
        cost_estimate=pl.CostEstimate(flops=flops, bytes_accessed=2**24, transcendentals=0),
    )(plan, t2_window, factors)
    return spread, norms


def home_kernel(plan, tiles, norms, residual, out, norms_out, wide):
    s = pl.program_id(0)
    for p in range(4):
        wide[p * 128:p * 128 + 128, :] = tiles[p // 2, p % 2, 0].astype(F32)
    keep = plan[4, s] == 1
    for a in range(VT):
        lanes = slice(a * 128, a * 128 + 128)
        ladder = wide[pl.ds(a, 4, stride=128), :]
        total = residual[0, :, lanes].astype(F32) + ladder
        out[0, :, lanes] = jnp.where(keep, total, 0.0).astype(BF)

    @pl.when(s == 0)
    def _():
        for i in range(2):
            for p in range(4):
                row = norms[pl.ds((p // 2) * 128 + plan[5, i] + p % 2, 1), :]
                norms_out[i, p] = jnp.max(row)


def at_home(plan, spread, norms, residual):
    return pl.pallas_call(
        home_kernel,
        out_shape=(
            jax.ShapeDtypeStruct(residual.shape, BF),
            jax.ShapeDtypeStruct((2, 4), F32),
        ),
        grid_spec=pltpu.PrefetchScalarGridSpec(
            num_scalar_prefetch=1,
            grid=(8,),
            in_specs=[
                pl.BlockSpec((2, 2, 1, VT, VT), lambda s, plan: (0, 0, plan[3, s], 0, 0)),
                pl.BlockSpec((256, 128), lambda s, plan: (0, 0)),
                pl.BlockSpec((1, 4, VT * VT), lambda s, plan: (s, 0, 0)),
            ],
            out_specs=[
                pl.BlockSpec((1, 4, VT * VT), lambda s, plan: (s, 0, 0)),
                pl.BlockSpec(memory_space=pltpu.SMEM),
            ],
            scratch_shapes=[pltpu.VMEM((4 * VT, VT), F32)],
        ),
    )(plan, spread, norms.reshape(256, 128), residual)


def plan_kernel(tile_mask, owner_slot, home_slot, plan):
    x, y, z, c = place()
    w = lax.axis_index("wide")
    n = 256
    r = lax.broadcasted_iota(I32, (n, n), 0)
    l = lax.broadcasted_iota(I32, (n, n), 1)
    eye = r == l

    def column(v):
        return jnp.sum(jnp.where(eye, v, 0), axis=1, keepdims=True)

    def pick(mask, v):
        return jnp.sum(jnp.where(mask, v, 0), axis=0, keepdims=True)

    mask_row, owner_row, home_row = tile_mask[...], owner_slot[...], home_slot[...]
    filled, home, owner = column(mask_row) == 1, column(home_row), column(owner_row)
    before = (mask_row == 1) & (home_row < home)
    where = jnp.sum(jnp.where(before, 1, 0), axis=1, keepdims=True)
    cell, turn = where & 15, where >> 4
    index = cell * 4 + turn
    match = filled & (index == l)
    ids = lax.broadcasted_iota(I32, (n, 1), 0)
    first_of = (ids * 4370) >> 16
    plan[0:1, :] = pick(match, first_of)
    plan[1:2, :] = pick(match, ids - first_of * NC)
    chips = pick(match, home >> 4)
    r16 = lax.broadcasted_iota(I32, (16, n), 0)
    t16 = lax.broadcasted_iota(I32, (16, n), 1)
    batch, k = r16 >> 2, r16 & 3
    by_y = (batch & 1) == 0
    group = jnp.where(by_y, y, z)
    far = (group + k) & 3
    target = jnp.where(by_y, z * 4 + far, far * 4 + y)
    hit = (t16 < FILLED) & ((t16 >> 4) == batch) & (((t16 >> 2) & 3) == group) & (chips == target)
    choice = jnp.sum(jnp.where(hit, t16 & 3, 0), axis=1, keepdims=True)
    plan[2:3, :] = pick(r16 == t16, choice)
    here = filled & (home == w * 8 + l) & (l < 8)
    plan[3:4, :] = pick(here, cell)
    plan[4:5, :] = pick(here, 1)
    batch_of, group_of = cell >> 2, cell & 3
    chip_of = jnp.where((batch_of & 1) == 0, turn * 4 + group_of, group_of * 4 + turn)
    plan[5:6, :] = pick(filled & (owner == w * 2 + l) & (l < 2), chip_of * 8 + 2 * batch_of)
    plan[6:8, :] = jnp.zeros((2, n), I32)


def make_plan(tile_mask, owner_slot, home_slot):
    rows = [jnp.pad(v, (0, 256 - NT)).reshape(1, 256) for v in (tile_mask, owner_slot, home_slot)]
    return pl.pallas_call(plan_kernel, out_shape=jax.ShapeDtypeStruct((8, 256), I32))(*rows)


def body(factors, t2_window, residual_in, tile_mask, owner_slot, home_slot):
    plan = make_plan(tile_mask, owner_slot, home_slot)
    spread, norms = ladders(plan, t2_window, factors)
    return at_home(plan, spread, norms, residual_in)


def solution(mesh):
    in_specs = (P(None, ("wide", "narrow"), None), P(), P("wide", "narrow", None), P(), P(), P())
    out_specs = (P("wide", "narrow", None), P("wide", "narrow"))
    return jax.shard_map(body, mesh=mesh, in_specs=in_specs, out_specs=out_specs, check_vma=False)
```

```python
import functools

import jax
import jax.numpy as jnp
from jax import lax
from jax.experimental import pallas as pl
from jax.experimental.pallas import tpu as pltpu
from jax.sharding import PartitionSpec as P

BF = jnp.bfloat16
F32 = jnp.float32
I32 = jnp.int32
MESH = pl.DeviceIdType.MESH
VT = 128
W = 15
NC = 15
NT = 225
ROWS = 56
KC = 1792
FILLED = 64
MAJOR = ("y", "z", "y", "z")
MINOR = ("z", "y", "z", "y")
UNITS = [(b, p) for p in (0, 1) for b in range(4)]
X_FIRST = {(0, 0), (1, 0), (0, 1), (1, 1)}


X_WHEN = {
    (0, 0): (0, 4, 11, 13),
    (1, 0): (1, 5, 12, 14),
    (0, 1): (8, 12, 17, 18),
    (1, 1): (9, 13, 17, 18),
}
M_GAP = 2
REST_GAP = 1


def place():
    w = lax.axis_index("wide")
    return lax.axis_index("narrow"), (w // 2) % 4, w // 8, w % 2


def at(x, y, z, c):
    return {"wide": z * 8 + y * 2 + c, "narrow": x}


def ladder_kernel(plan, t2, own_rows, spread, norms, other_rows, *scratch):
    weights, f2, f1t, y_buf, out, raw, r1, r2, r3 = scratch[:9]
    done = dict(zip(UNITS, scratch[9:17]))
    (squares, ex_s, ex_r, ld_s, s1_s, s1_r, s2_s, s2_r, s3_s, s3_r, ag_s, ag_r, aa_s, aa_r, co_s, co_r, st_s,
     nz_s, nz_r, ny_s, ny_r, nc_s, nc_r, nl_s) = scratch[17:]
    x, y, z, c = place()
    ring = {
        "x": (x, [at((x + k) % 4, y, z, c) for k in range(4)]),
        "y": (y, [at(x, (y + k) % 4, z, c) for k in range(4)]),
        "z": (z, [at(x, y, (z + k) % 4, c) for k in range(4)]),
    }
    partner = at(x, y, z, 1 - c)

    barrier = pltpu.get_barrier_semaphore()
    greeted = [partner] + [ring[a][1][k] for a in "xyz" for k in (1, 2, 3)]
    for device in greeted:
        pl.semaphore_signal(barrier, inc=1, device_id=device, device_id_type=MESH)
    pl.semaphore_wait(barrier, len(greeted))

    def remote(src, dst, s_sem, r_sem, device):
        return pltpu.make_async_remote_copy(
            src_ref=src, dst_ref=dst, send_sem=s_sem, recv_sem=r_sem, device_id=device, device_id_type=MESH
        )

    def exchange(i):
        return remote(own_rows.at[i], other_rows.at[i], ex_s.at[i], ex_r.at[i], partner)

    def start_exchange(i, _):
        exchange(i).start()
        return 0

    lax.fori_loop(0, NC, start_exchange, 0)

    def load(which, i):
        src = (own_rows, other_rows)[which]
        return pltpu.make_async_copy(src.at[i], raw.at[which, i % 3], ld_s.at[which, i % 3])

    load(0, 0).start()
    load(0, 1).start()

    row = lax.broadcasted_iota(I32, (256, W), 0)
    col = lax.broadcasted_iota(I32, (256, W), 1)
    widen = (row // 16 == col).astype(F32).astype(BF)
    row2 = lax.broadcasted_iota(I32, (256, 256), 0)
    col2 = lax.broadcasted_iota(I32, (256, 256), 1)
    same = row2 % 16 == col2 % 16
    for s in range(4):
        for slot in range(2):
            ahead = (2, 1, 3, 0)[(s % 2) * 2 + slot]
            pair = ((x + ahead) % 4) * 4 + c * 2 + s // 2
            tall = jnp.dot(widen, t2[pair], preferred_element_type=F32).astype(BF)
            full = lax.dot_general(tall, widen, (((1,), (1,)), ((), ())), preferred_element_type=F32)
            weights[s, slot * 256:slot * 256 + 256, :] = jnp.where(same, full, 0.0).astype(BF)
    f2[52, :, 128:256] = jnp.zeros((256, 128), BF)

    def assemble(i, blocks):
        slot = i % 3
        for blk in blocks:
            parts = []
            for d in range(W):
                lanes = slice(d * 128, d * 128 + 128)
                if blk < 6:
                    r0 = (blk % 3) * 16
                    parts.append(raw[blk // 3, slot, r0:r0 + 16, lanes])
                else:
                    parts.append(
                        jnp.concatenate([raw[0, slot, 48:56, lanes], raw[1, slot, 48:56, lanes]], axis=0)
                    )
            parts.append(jnp.zeros((16, 128), BF))
            block = jnp.concatenate(parts, axis=0)
            f1t[i, :, blk * 256:blk * 256 + 256] = block.T
            if blk < 6:
                f2[i * 3 + blk // 2, :, (blk % 2) * 128:(blk % 2) * 128 + 128] = block
            else:
                f2[45 + i // 2, :, pl.ds(pl.multiple_of((i % 2) * 128, 128), 128)] = block

    def assemble_own(i, _):
        @pl.when(i + 2 < NC)
        def _():
            load(0, i + 2).start()

        load(0, i).wait()
        assemble(i, (0, 1, 2))
        return 0

    lax.fori_loop(0, NC, assemble_own, 0)

    def put_block(o, i, blk, half):
        rows = slice(blk * 256, blk * 256 + 256)
        for slot in range(2):
            y_buf[i, rows, slot * 128:slot * 128 + 128] = o[slot * 256:slot * 256 + 256, half * 128:half * 128 + 128]

    def amplitude_pairs(s, pairs):
        def cluster(n, _):
            for u in range(3):
                for j in pairs:
                    i = n * 3 + u
                    o = jnp.dot(weights[s], f2[i * 3 + j], preferred_element_type=F32).astype(BF)
                    for half in range(2):
                        put_block(o, i, 2 * j + half, half)
            return 0

        lax.fori_loop(0, NC // 3, cluster, 0)

    def amplitude_last(s):
        for i in range(8):
            o = jnp.dot(weights[s], f2[45 + i], preferred_element_type=F32).astype(BF)
            for half in range(2):
                if 2 * i + half < NC:
                    put_block(o, 2 * i + half, 6, half)

    amplitude_pairs(0, (0,))

    def start_both(i):
        load(0, i).start()
        exchange(i).wait_recv()
        load(1, i).start()

    start_both(0)
    start_both(1)

    def assemble_other(i, _):
        @pl.when(i + 2 < NC)
        def _():
            start_both(i + 2)

        load(0, i).wait()
        load(1, i).wait()
        assemble(i, (3, 4, 5, 6))
        return 0

    lax.fori_loop(0, NC, assemble_other, 0)

    def compute(s, b):
        for i in range(16):
            t = b * 16 + i
            o = jnp.dot(f1t[plan[0, t]], y_buf[plan[1, t]], preferred_element_type=F32).astype(BF)
            out[s, 0, t] = o[:, :128]
            out[s, 1, t] = o[:, 128:]

    def add_tiles(dst, terms, n):
        def one(i, _):
            total = dst.at[i][...].astype(F32)
            for term in terms:
                total = total + term.at[i][...].astype(F32)
            dst.at[i][...] = total.astype(BF)
            return 0

        lax.fori_loop(0, n, one, 0)

    def route(way, kind):
        return (2 if kind == 0 else (3 if way else 1)), (1 - way if kind == 1 else way)

    def corner(b):
        return 16 * b, ring[MAJOR[b]][0], ring[MINOR[b]][0]

    def number(unit):
        return unit[1] * 4 + unit[0]

    PLANE = {2: (0, 0), 1: (0, 1), 3: (1, 0), 0: (1, 1)}

    def x_part(unit, k, half):
        b, p = unit
        s, slot = PLANE[k]
        return out.at[2 * p + s, slot, 16 * b + 8 * half:16 * b + 8 * half + 8]

    def x_put(unit, way, kind):
        u = number(unit)
        return remote(
            x_part(unit, *route(way, kind)), r1.at[u, way, kind], s1_s.at[u, way, kind, 0],
            s1_r.at[u, way, kind, 0], ring["x"][1][3 if way else 1],
        )

    def x_begin(unit):
        x_put(unit, 0, 0).start()
        x_put(unit, 1, 0).start()
        x_put(unit, 0, 1).start()

    def x_pass(unit):
        x_put(unit, 1, 1).start()
        for way in (0, 1):
            x_put(unit, way, 0).wait_recv()
            add_tiles(x_part(unit, *route(way, 2)), [r1.at[number(unit), way, 0]], 8)
            x_put(unit, way, 2).start()

    def x_sum(unit):
        u = number(unit)
        for way in (0, 1):
            for kind in (1, 2):
                x_put(unit, way, kind).wait_recv()
        for half in range(2):
            add_tiles(x_part(unit, 0, half), [r1.at[u, half, 2], r1.at[u, 1 - half, 1]], 8)
        for k in (2, 1, 3):
            x2_put(unit, k).start()

    def x2_part(unit, k):
        b, p = unit
        base, hi, lo = corner(b)
        return out.at[2 * p + 1, 1, pl.ds(base + ((hi + k) % 4) * 4, 4)]

    def x2_put(unit, k):
        u = number(unit)
        return remote(
            x2_part(unit, k), r2.at[u, k - 1], s2_s.at[u, k - 1, 0], s2_r.at[u, k - 1, 0], ring[MAJOR[unit[0]]][1][k]
        )

    def x2_sum(unit):
        u = number(unit)
        for k in (1, 2, 3):
            x2_put(unit, k).wait_recv()
        add_tiles(x2_part(unit, 0), [r2.at[u, k] for k in range(3)], 4)
        last_send(unit)

    def m_part(unit, s, k, half):
        b, p = unit
        base, hi, lo = corner(b)
        return out.at[2 * p + s, :, pl.ds(base + ((hi + k) % 4) * 4 + 2 * half, 2)]

    def m_land(unit, s, way, kind):
        return r1.at[number(unit), way, kind, 4 * s:4 * s + 4]

    def m_put(unit, s, slot, way, kind):
        u = number(unit)
        return remote(
            m_part(unit, s, *route(way, kind)).at[slot], m_land(unit, s, way, kind).at[2 * slot:2 * slot + 2],
            s1_s.at[u, way, kind, 2 * s + slot], s1_r.at[u, way, kind, 2 * s + slot],
            ring[MAJOR[unit[0]]][1][3 if way else 1],
        )

    def m_begin(unit, s):
        for kind in (0, 1):
            for way in (0, 1):
                for slot in range(2):
                    m_put(unit, s, slot, way, kind).start()

    def m_pass(unit, s):
        for way in (0, 1):
            for slot in range(2):
                m_put(unit, s, slot, way, 0).wait_recv()
                add_tiles(
                    m_part(unit, s, *route(way, 2)).at[slot], [m_land(unit, s, way, 0).at[2 * slot:2 * slot + 2]], 2
                )
                m_put(unit, s, slot, way, 2).start()

    def m_sum(unit, s):
        for way in (0, 1):
            for kind in (1, 2):
                for slot in range(2):
                    m_put(unit, s, slot, way, kind).wait_recv()
        for half in range(2):
            for slot in range(2):
                two = slice(2 * slot, 2 * slot + 2)
                add_tiles(
                    m_part(unit, s, 0, half).at[slot],
                    [m_land(unit, s, half, 2).at[two], m_land(unit, s, 1 - half, 1).at[two]], 2,
                )
        for k in (2, 1, 3):
            m2_put(unit, s, k).start()

    def m2_part(unit, s, k):
        b, p = unit
        base, hi, lo = corner(b)
        return out.at[2 * p + s, :, base + hi * 4 + (lo + k) % 4]

    def m2_put(unit, s, k):
        u = number(unit)
        return remote(
            m2_part(unit, s, k), r2.at[u, k - 1, 2 * s:2 * s + 2], s2_s.at[u, k - 1, s], s2_r.at[u, k - 1, s],
            ring[MINOR[unit[0]]][1][k],
        )

    def m2_sum(unit, s):
        u = number(unit)
        for k in (1, 2, 3):
            m2_put(unit, s, k).wait_recv()
        add_tiles(m2_part(unit, s, 0), [r2.at[u, k, 2 * s:2 * s + 2] for k in range(3)], 2)
        if s == 1:
            last_send(unit)

    def last_part(unit, k):
        b, p = unit
        base, hi, lo = corner(b)
        if unit in X_FIRST:
            return out.at[2 * p + 1, 1, base + hi * 4 + (lo + k) % 4]
        s, slot = PLANE[k]
        return out.at[2 * p + s, slot, base + hi * 4 + lo]

    def last_put(unit, k):
        u = number(unit)
        axis = MINOR[unit[0]] if unit in X_FIRST else "x"
        return remote(last_part(unit, k), r3.at[u, k - 1], s3_s.at[u, k - 1], s3_r.at[u, k - 1], ring[axis][1][k])

    def last_send(unit):
        for k in (2, 1, 3):
            last_put(unit, k).start()

    def last_sum(unit):
        b, p = unit
        u = number(unit)
        base, hi, lo = corner(b)
        for k in (1, 2, 3):
            last_put(unit, k).wait_recv()
        total = last_part(unit, 0)[...].astype(F32)
        for k in range(3):
            total = total + r3[u, k].astype(F32)
        tile = total.astype(BF)
        done[unit][lo] = tile
        for k in (2, 1, 3):
            share(unit, k).start()
        value = tile.astype(F32)
        mean = jnp.sum(value * value, keepdims=True) * (1.0 / (VT * VT))
        squares[c, z, y, 2 * b + p:2 * b + p + 1, :] = jnp.broadcast_to(mean, (1, 128))

    def share(unit, k):
        u = number(unit)
        lo = corner(unit[0])[2]
        return remote(
            done[unit].at[lo], done[unit].at[lo], ag_s.at[u, k - 1], ag_r.at[u, k - 1], ring[MINOR[unit[0]]][1][k]
        )

    def packed(unit, k):
        return r1.at[number(unit), 0, 0, k]

    def deliver(unit, k):
        b, p = unit
        u = number(unit)
        cell = spread.at[c, p, 4 * b + corner(b)[1]]
        if k == 0:
            return pltpu.make_async_copy(packed(unit, 0), cell, st_s.at[u])
        return remote(packed(unit, k), cell, aa_s.at[u, k - 1], aa_r.at[u, k - 1], ring[MAJOR[b]][1][k])

    def handout(unit):
        b, p = unit
        for k in (1, 2, 3):
            share(unit, k).wait_recv()
        for k in (2, 1, 3, 0):
            r1[number(unit), 0, 0, k] = done[unit][plan[2, 4 * b + k]]
            deliver(unit, k).start()

    def core_copy(unit):
        b, p = unit
        rows = spread.at[c, p, 4 * b:4 * b + 4]
        return remote(rows, rows, co_s.at[number(unit)], co_r.at[number(unit)], partner)

    def finish(unit):
        deliver(unit, 0).wait()
        for k in (1, 2, 3):
            deliver(unit, k).wait_recv()
        core_copy(unit).start()

    def phases(unit):
        bind = functools.partial
        if unit in X_FIRST:
            first = [bind(f, unit) for f in (x_begin, x_pass, x_sum, x2_sum)]
        else:
            acts = (m_begin, m_pass, m_sum, m2_sum)
            first = [[bind(f, unit, s) for f in acts] for s in (0, 1)]
        return first, [bind(f, unit) for f in (last_sum, handout, finish)]

    def norms_z(k):
        part = squares.at[c, z, y]
        return remote(part, part, nz_s.at[k - 1], nz_r.at[k - 1], ring["z"][1][k])

    def norms_y(k):
        part = squares.at[c, :, y]
        return remote(part, part, ny_s.at[k - 1], ny_r.at[k - 1], ring["y"][1][k])

    def norms_core():
        return remote(squares.at[c], norms.at[c], nc_s, nc_r, partner)

    def norms_keep():
        return pltpu.make_async_copy(squares.at[c], norms.at[c], nl_s)

    def norms_begin():
        for k in (1, 2, 3):
            norms_z(k).start()

    def norms_next():
        for k in (1, 2, 3):
            norms_z(k).wait_recv()
        for k in (1, 2, 3):
            norms_y(k).start()

    def norms_last():
        for k in (1, 2, 3):
            norms_y(k).wait_recv()
        norms_core().start()
        norms_keep().start()

    events = []
    for unit in UNITS:
        b, p = unit
        first, rest = phases(unit)
        if unit in X_FIRST:
            when = X_WHEN[unit]
            last = when[-1]
            events += list(zip(when, first))
        else:
            for s in (0, 1):
                start = 8 * p + 4 * s + b
                when = [start + n * M_GAP for n in range(4)]
                if start + M_GAP > 15:
                    when = [start] + [max(16, start) + n for n in range(3)]
                else:
                    when = [w if w <= 15 else 16 + n - [v <= 15 for v in when].count(True) for n, w in enumerate(when)]
                last = when[-1]
                events += list(zip(when, first[s]))
        for act in rest:
            last = last + REST_GAP if last + REST_GAP <= 15 else max(16, last + 1)
            events.append((last, act))
    end = max(when for when, act in events)
    norm_at = end - 2
    events += [(norm_at + n, act) for n, act in enumerate((norms_begin, norms_next, norms_last))]
    events = sorted(enumerate(events), key=lambda e: (e[1][0], e[0]))
    by_slot = {}
    for _, (when, act) in events:
        by_slot.setdefault(when, []).append(act)

    def step(s, _):
        @pl.when(s > 0)
        def _():
            amplitude_pairs(s, (0,))

        amplitude_pairs(s, (1, 2))
        amplitude_last(s)
        for b in range(4):
            compute(s, b)
            for k in range(4):
                acts = by_slot.get(4 * k + b, [])
                if acts:
                    @pl.when(s == k)
                    def _():
                        for act in acts:
                            act()
        return 0

    lax.fori_loop(0, 4, step, 0)
    for when in sorted(by_slot):
        if when > 15:
            for act in by_slot[when]:
                act()

    for unit in UNITS:
        core_copy(unit).wait_recv()
    norms_keep().wait()
    norms_core().wait_recv()

    def wait_exchange(i, _):
        exchange(i).wait_send()
        return 0

    lax.fori_loop(0, NC, wait_exchange, 0)
    for unit in UNITS:
        for way in (0, 1):
            for kind in range(3):
                if unit in X_FIRST:
                    x_put(unit, way, kind).wait_send()
                else:
                    for s in (0, 1):
                        for slot in (0, 1):
                            m_put(unit, s, slot, way, kind).wait_send()
        for k in (1, 2, 3):
            if unit in X_FIRST:
                x2_put(unit, k).wait_send()
            else:
                for s in (0, 1):
                    m2_put(unit, s, k).wait_send()
            last_put(unit, k).wait_send()
            share(unit, k).wait_send()
            deliver(unit, k).wait_send()
        core_copy(unit).wait_send()
    for k in (1, 2, 3):
        norms_z(k).wait_send()
        norms_y(k).wait_send()
    norms_core().wait_send()


def ladders(plan, t2_window, factors):
    dma = pltpu.SemaphoreType.DMA
    any_space = pl.BlockSpec(memory_space=pl.ANY)
    smem = pl.BlockSpec(memory_space=pltpu.SMEM)
    vmem = pl.BlockSpec(memory_space=pltpu.VMEM)
    flops = 2 * FILLED * 8 * VT * VT * KC
    spread, norms, _ = pl.pallas_call(
        ladder_kernel,
        out_shape=(
            jax.ShapeDtypeStruct((2, 2, 16, VT, VT), BF),
            jax.ShapeDtypeStruct((2, 4, 4, 8, 128), F32),
            jax.ShapeDtypeStruct(factors.shape, BF),
        ),
        in_specs=[smem, vmem, any_space],
        out_specs=(any_space, any_space, any_space),
        scratch_shapes=[
            pltpu.VMEM((4, 512, 256), BF),
            pltpu.VMEM((53, 256, 256), BF),
            pltpu.VMEM((NC, VT, KC), BF),
            pltpu.VMEM((NC, KC, 256), BF),
            pltpu.VMEM((4, 2, FILLED, VT, VT), BF),
            pltpu.VMEM((2, 3, ROWS, W * VT), BF),
            pltpu.VMEM((8, 2, 3, 8, VT, VT), BF),
            pltpu.VMEM((8, 3, 4, VT, VT), BF),
            pltpu.VMEM((8, 3, VT, VT), BF),
        ]
        + [pltpu.VMEM((4, VT, VT), BF) for _ in UNITS]
        + [
            pltpu.VMEM((2, 4, 4, 8, 128), F32),
            dma((NC,)), dma((NC,)), dma((2, 3)),
            dma((8, 2, 3, 4)), dma((8, 2, 3, 4)), dma((8, 3, 2)), dma((8, 3, 2)), dma((8, 3)), dma((8, 3)),
            dma((8, 3)), dma((8, 3)), dma((8, 3)), dma((8, 3)), dma((8,)), dma((8,)), dma((8,)),
            dma((3,)), dma((3,)), dma((3,)), dma((3,)), dma, dma, dma,
        ],
        compiler_params=pltpu.CompilerParams(
            collective_id=0, has_side_effects=True, vmem_limit_bytes=63 * 2**20
        ),
        cost_estimate=pl.CostEstimate(flops=flops, bytes_accessed=2**24, transcendentals=0),
    )(plan, t2_window, factors)
    return spread, norms


def home_kernel(plan, tiles, norms, residual, out, norms_out, wide):
    s = pl.program_id(0)
    for p in range(4):
        wide[p * 128:p * 128 + 128, :] = tiles[p // 2, p % 2, 0].astype(F32)
    keep = plan[4, s] == 1
    for a in range(VT):
        lanes = slice(a * 128, a * 128 + 128)
        ladder = wide[pl.ds(a, 4, stride=128), :]
        total = residual[0, :, lanes].astype(F32) + ladder
        out[0, :, lanes] = jnp.where(keep, total, 0.0).astype(BF)

    @pl.when(s == 0)
    def _():
        for i in range(2):
            for p in range(4):
                row = norms[pl.ds((p // 2) * 128 + plan[5, i] + p % 2, 1), :]
                norms_out[i, p] = jnp.max(row)


def at_home(plan, spread, norms, residual):
    return pl.pallas_call(
        home_kernel,
        out_shape=(
            jax.ShapeDtypeStruct(residual.shape, BF),
            jax.ShapeDtypeStruct((2, 4), F32),
        ),
        grid_spec=pltpu.PrefetchScalarGridSpec(
            num_scalar_prefetch=1,
            grid=(8,),
            in_specs=[
                pl.BlockSpec((2, 2, 1, VT, VT), lambda s, plan: (0, 0, plan[3, s], 0, 0)),
                pl.BlockSpec((256, 128), lambda s, plan: (0, 0)),
                pl.BlockSpec((1, 4, VT * VT), lambda s, plan: (s, 0, 0)),
            ],
            out_specs=[
                pl.BlockSpec((1, 4, VT * VT), lambda s, plan: (s, 0, 0)),
                pl.BlockSpec(memory_space=pltpu.SMEM),
            ],
            scratch_shapes=[pltpu.VMEM((4 * VT, VT), F32)],
        ),
    )(plan, spread, norms.reshape(256, 128), residual)


def plan_kernel(rows, plan):
    x, y, z, c = place()
    w = lax.axis_index("wide")
    n = 256
    r = lax.broadcasted_iota(I32, (n, n), 0)
    l = lax.broadcasted_iota(I32, (n, n), 1)
    eye = r == l

    def column(v):
        return jnp.sum(jnp.where(eye, v, 0), axis=1, keepdims=True)

    def pick(mask, v):
        return jnp.sum(jnp.where(mask, v, 0), axis=0, keepdims=True)

    mask_row, owner_row, home_row = rows[0:1, :], rows[1:2, :], rows[2:3, :]
    filled, home, owner = column(mask_row) == 1, column(home_row), column(owner_row)
    before = (mask_row == 1) & (home_row < home)
    where = jnp.sum(jnp.where(before, 1, 0), axis=1, keepdims=True)
    cell, turn = where & 15, where >> 4
    index = cell * 4 + turn
    match = filled & (index == l)
    ids = lax.broadcasted_iota(I32, (n, 1), 0)
    first_of = (ids * 4370) >> 16
    plan[0:1, :] = pick(match, first_of)
    plan[1:2, :] = pick(match, ids - first_of * NC)
    chips = pick(match, home >> 4)
    r16 = lax.broadcasted_iota(I32, (16, n), 0)
    t16 = lax.broadcasted_iota(I32, (16, n), 1)
    batch, k = r16 >> 2, r16 & 3
    by_y = (batch & 1) == 0
    group = jnp.where(by_y, y, z)
    far = (group + k) & 3
    target = jnp.where(by_y, z * 4 + far, far * 4 + y)
    hit = (t16 < FILLED) & ((t16 >> 4) == batch) & (((t16 >> 2) & 3) == group) & (chips == target)
    choice = jnp.sum(jnp.where(hit, t16 & 3, 0), axis=1, keepdims=True)
    plan[2:3, :] = pick(r16 == t16, choice)
    here = filled & (home == w * 8 + l) & (l < 8)
    plan[3:4, :] = pick(here, cell)
    plan[4:5, :] = pick(here, 1)
    batch_of, group_of = cell >> 2, cell & 3
    chip_of = jnp.where((batch_of & 1) == 0, turn * 4 + group_of, group_of * 4 + turn)
    plan[5:6, :] = pick(filled & (owner == w * 2 + l) & (l < 2), chip_of * 8 + 2 * batch_of)
    plan[6:8, :] = jnp.zeros((2, n), I32)


def make_plan(tile_mask, owner_slot, home_slot):
    rows = jnp.pad(jnp.stack([tile_mask, owner_slot, home_slot]), ((0, 5), (0, 256 - NT)))
    return pl.pallas_call(plan_kernel, out_shape=jax.ShapeDtypeStruct((8, 256), I32))(rows)


def body(factors, t2_window, residual_in, tile_mask, owner_slot, home_slot):
    plan = make_plan(tile_mask, owner_slot, home_slot)
    spread, norms = ladders(plan, t2_window, factors)
    return at_home(plan, spread, norms, residual_in)


def solution(mesh):
    in_specs = (P(None, ("wide", "narrow"), None), P(), P("wide", "narrow", None), P(), P(), P())
    out_specs = (P("wide", "narrow", None), P("wide", "narrow"))
    return jax.shard_map(body, mesh=mesh, in_specs=in_specs, out_specs=out_specs, check_vma=False)
```

```python
import functools

import jax
import jax.numpy as jnp
from jax import lax
from jax.experimental import pallas as pl
from jax.experimental.pallas import tpu as pltpu
from jax.sharding import PartitionSpec as P

BF = jnp.bfloat16
F32 = jnp.float32
I32 = jnp.int32
MESH = pl.DeviceIdType.MESH
VT = 128
W = 15
NC = 15
NT = 225
ROWS = 56
KC = 1792
FILLED = 64
MAJOR = ("y", "z", "y", "z")
MINOR = ("z", "y", "z", "y")
UNITS = [(b, p) for p in (0, 1) for b in range(4)]
X_FIRST = {(0, 0), (1, 0), (0, 1), (1, 1)}


X_WHEN = {(0, 0): (0, 4, 10, 12), (1, 0): (1, 5, 11, 13), (0, 1): (8, 12, 17, 18), (1, 1): (9, 13, 17, 18)}
M_GAP = 2
REST_GAP = 1


def place():
    w = lax.axis_index("wide")
    return lax.axis_index("narrow"), (w // 2) % 4, w // 8, w % 2


def at(x, y, z, c):
    return {"wide": z * 8 + y * 2 + c, "narrow": x}


def ladder_kernel(plan, t2, own_rows, spread, norms, other_rows, *scratch):
    weights, f2, f1t, y_buf, out, raw, r1, r2, r3 = scratch[:9]
    done = dict(zip(UNITS, scratch[9:17]))
    (squares, ex_s, ex_r, ld_s, s1_s, s1_r, s2_s, s2_r, s3_s, s3_r, ag_s, ag_r, aa_s, aa_r, co_s, co_r, st_s,
     nz_s, nz_r, ny_s, ny_r, nc_s, nc_r, nl_s) = scratch[17:]
    x, y, z, c = place()
    ring = {
        "x": (x, [at((x + k) % 4, y, z, c) for k in range(4)]),
        "y": (y, [at(x, (y + k) % 4, z, c) for k in range(4)]),
        "z": (z, [at(x, y, (z + k) % 4, c) for k in range(4)]),
    }
    partner = at(x, y, z, 1 - c)

    barrier = pltpu.get_barrier_semaphore()
    greeted = [partner] + [ring[a][1][k] for a in "xyz" for k in (1, 2, 3)]
    for device in greeted:
        pl.semaphore_signal(barrier, inc=1, device_id=device, device_id_type=MESH)
    pl.semaphore_wait(barrier, len(greeted))

    def remote(src, dst, s_sem, r_sem, device):
        return pltpu.make_async_remote_copy(
            src_ref=src, dst_ref=dst, send_sem=s_sem, recv_sem=r_sem, device_id=device, device_id_type=MESH
        )

    def exchange(i):
        return remote(own_rows.at[i], other_rows.at[i], ex_s.at[i], ex_r.at[i], partner)

    def start_exchange(i, _):
        exchange(i).start()
        return 0

    lax.fori_loop(0, NC, start_exchange, 0)

    def load(which, i):
        src = (own_rows, other_rows)[which]
        return pltpu.make_async_copy(src.at[i], raw.at[which, i % 3], ld_s.at[which, i % 3])

    load(0, 0).start()
    load(0, 1).start()

    row = lax.broadcasted_iota(I32, (256, W), 0)
    col = lax.broadcasted_iota(I32, (256, W), 1)
    widen = (row // 16 == col).astype(F32).astype(BF)
    row2 = lax.broadcasted_iota(I32, (256, 256), 0)
    col2 = lax.broadcasted_iota(I32, (256, 256), 1)
    same = row2 % 16 == col2 % 16
    for s in range(4):
        for slot in range(2):
            ahead = (2, 1, 3, 0)[(s % 2) * 2 + slot]
            pair = ((x + ahead) % 4) * 4 + c * 2 + s // 2
            tall = jnp.dot(widen, t2[pair], preferred_element_type=F32).astype(BF)
            full = lax.dot_general(tall, widen, (((1,), (1,)), ((), ())), preferred_element_type=F32)
            weights[s, slot * 256:slot * 256 + 256, :] = jnp.where(same, full, 0.0).astype(BF)
    f2[52, :, 128:256] = jnp.zeros((256, 128), BF)

    def assemble(i, blocks):
        slot = i % 3
        for blk in blocks:
            parts = []
            for d in range(W):
                lanes = slice(d * 128, d * 128 + 128)
                if blk < 6:
                    r0 = (blk % 3) * 16
                    parts.append(raw[blk // 3, slot, r0:r0 + 16, lanes])
                else:
                    parts.append(
                        jnp.concatenate([raw[0, slot, 48:56, lanes], raw[1, slot, 48:56, lanes]], axis=0)
                    )
            parts.append(jnp.zeros((16, 128), BF))
            block = jnp.concatenate(parts, axis=0)
            f1t[i, :, blk * 256:blk * 256 + 256] = block.T
            if blk < 6:
                f2[i * 3 + blk // 2, :, (blk % 2) * 128:(blk % 2) * 128 + 128] = block
            else:
                f2[45 + i // 2, :, pl.ds(pl.multiple_of((i % 2) * 128, 128), 128)] = block

    def assemble_own(i, _):
        @pl.when(i + 2 < NC)
        def _():
            load(0, i + 2).start()

        load(0, i).wait()
        assemble(i, (0, 1, 2))
        return 0

    lax.fori_loop(0, NC, assemble_own, 0)

    def put_block(o, i, blk, half):
        rows = slice(blk * 256, blk * 256 + 256)
        for slot in range(2):
            y_buf[i, rows, slot * 128:slot * 128 + 128] = o[slot * 256:slot * 256 + 256, half * 128:half * 128 + 128]

    def amplitude_pairs(s, pairs):
        def cluster(n, _):
            for u in range(3):
                for j in pairs:
                    i = n * 3 + u
                    o = jnp.dot(weights[s], f2[i * 3 + j], preferred_element_type=F32).astype(BF)
                    for half in range(2):
                        put_block(o, i, 2 * j + half, half)
            return 0

        lax.fori_loop(0, NC // 3, cluster, 0)

    def amplitude_last(s):
        for i in range(8):
            o = jnp.dot(weights[s], f2[45 + i], preferred_element_type=F32).astype(BF)
            for half in range(2):
                if 2 * i + half < NC:
                    put_block(o, 2 * i + half, 6, half)

    amplitude_pairs(0, (0,))

    def start_both(i):
        load(0, i).start()
        exchange(i).wait_recv()
        load(1, i).start()

    start_both(0)
    start_both(1)

    def assemble_other(i, _):
        @pl.when(i + 2 < NC)
        def _():
            start_both(i + 2)

        load(0, i).wait()
        load(1, i).wait()
        assemble(i, (3, 4, 5, 6))
        return 0

    lax.fori_loop(0, NC, assemble_other, 0)

    def compute(s, b):
        for i in range(16):
            t = b * 16 + i
            o = jnp.dot(f1t[plan[0, t]], y_buf[plan[1, t]], preferred_element_type=F32).astype(BF)
            out[s, 0, t] = o[:, :128]
            out[s, 1, t] = o[:, 128:]

    def add_tiles(dst, terms, n):
        def one(i, _):
            total = dst.at[i][...].astype(F32)
            for term in terms:
                total = total + term.at[i][...].astype(F32)
            dst.at[i][...] = total.astype(BF)
            return 0

        lax.fori_loop(0, n, one, 0)

    def route(way, kind):
        return (2 if kind == 0 else (3 if way else 1)), (1 - way if kind == 1 else way)

    def corner(b):
        return 16 * b, ring[MAJOR[b]][0], ring[MINOR[b]][0]

    def number(unit):
        return unit[1] * 4 + unit[0]

    PLANE = {2: (0, 0), 1: (0, 1), 3: (1, 0), 0: (1, 1)}

    def x_part(unit, k, half):
        b, p = unit
        s, slot = PLANE[k]
        return out.at[2 * p + s, slot, 16 * b + 8 * half:16 * b + 8 * half + 8]

    def x_put(unit, way, kind):
        u = number(unit)
        return remote(
            x_part(unit, *route(way, kind)), r1.at[u, way, kind], s1_s.at[u, way, kind, 0],
            s1_r.at[u, way, kind, 0], ring["x"][1][3 if way else 1],
        )

    def x_begin(unit):
        x_put(unit, 0, 0).start()
        x_put(unit, 1, 0).start()
        x_put(unit, 0, 1).start()

    def x_pass(unit):
        x_put(unit, 1, 1).start()
        for way in (0, 1):
            x_put(unit, way, 0).wait_recv()
            add_tiles(x_part(unit, *route(way, 2)), [r1.at[number(unit), way, 0]], 8)
            x_put(unit, way, 2).start()

    def x_sum(unit):
        u = number(unit)
        for way in (0, 1):
            for kind in (1, 2):
                x_put(unit, way, kind).wait_recv()
        for half in range(2):
            add_tiles(x_part(unit, 0, half), [r1.at[u, half, 2], r1.at[u, 1 - half, 1]], 8)
        for k in (2, 1, 3):
            x2_put(unit, k).start()

    def x2_part(unit, k):
        b, p = unit
        base, hi, lo = corner(b)
        return out.at[2 * p + 1, 1, pl.ds(base + ((hi + k) % 4) * 4, 4)]

    def x2_put(unit, k):
        u = number(unit)
        return remote(
            x2_part(unit, k), r2.at[u, k - 1], s2_s.at[u, k - 1, 0], s2_r.at[u, k - 1, 0], ring[MAJOR[unit[0]]][1][k]
        )

    def x2_sum(unit):
        u = number(unit)
        for k in (1, 2, 3):
            x2_put(unit, k).wait_recv()
        add_tiles(x2_part(unit, 0), [r2.at[u, k] for k in range(3)], 4)
        last_send(unit)

    def m_part(unit, s, k, half):
        b, p = unit
        base, hi, lo = corner(b)
        return out.at[2 * p + s, :, pl.ds(base + ((hi + k) % 4) * 4 + 2 * half, 2)]

    def m_land(unit, s, way, kind):
        return r1.at[number(unit), way, kind, 4 * s:4 * s + 4]

    def m_put(unit, s, slot, way, kind):
        u = number(unit)
        return remote(
            m_part(unit, s, *route(way, kind)).at[slot], m_land(unit, s, way, kind).at[2 * slot:2 * slot + 2],
            s1_s.at[u, way, kind, 2 * s + slot], s1_r.at[u, way, kind, 2 * s + slot],
            ring[MAJOR[unit[0]]][1][3 if way else 1],
        )

    def m_begin(unit, s):
        for kind in (0, 1):
            for way in (0, 1):
                for slot in range(2):
                    m_put(unit, s, slot, way, kind).start()

    def m_pass(unit, s):
        for way in (0, 1):
            for slot in range(2):
                m_put(unit, s, slot, way, 0).wait_recv()
                add_tiles(
                    m_part(unit, s, *route(way, 2)).at[slot], [m_land(unit, s, way, 0).at[2 * slot:2 * slot + 2]], 2
                )
                m_put(unit, s, slot, way, 2).start()

    def m_sum(unit, s):
        for way in (0, 1):
            for kind in (1, 2):
                for slot in range(2):
                    m_put(unit, s, slot, way, kind).wait_recv()
        for half in range(2):
            for slot in range(2):
                two = slice(2 * slot, 2 * slot + 2)
                add_tiles(
                    m_part(unit, s, 0, half).at[slot],
                    [m_land(unit, s, half, 2).at[two], m_land(unit, s, 1 - half, 1).at[two]], 2,
                )
        for k in (2, 1, 3):
            m2_put(unit, s, k).start()

    def m2_part(unit, s, k):
        b, p = unit
        base, hi, lo = corner(b)
        return out.at[2 * p + s, :, base + hi * 4 + (lo + k) % 4]

    def m2_put(unit, s, k):
        u = number(unit)
        return remote(
            m2_part(unit, s, k), r2.at[u, k - 1, 2 * s:2 * s + 2], s2_s.at[u, k - 1, s], s2_r.at[u, k - 1, s],
            ring[MINOR[unit[0]]][1][k],
        )

    def m2_sum(unit, s):
        u = number(unit)
        for k in (1, 2, 3):
            m2_put(unit, s, k).wait_recv()
        add_tiles(m2_part(unit, s, 0), [r2.at[u, k, 2 * s:2 * s + 2] for k in range(3)], 2)
        if s == 1:
            last_send(unit)

    def last_part(unit, k):
        b, p = unit
        base, hi, lo = corner(b)
        if unit in X_FIRST:
            return out.at[2 * p + 1, 1, base + hi * 4 + (lo + k) % 4]
        s, slot = PLANE[k]
        return out.at[2 * p + s, slot, base + hi * 4 + lo]

    def last_put(unit, k):
        u = number(unit)
        axis = MINOR[unit[0]] if unit in X_FIRST else "x"
        return remote(last_part(unit, k), r3.at[u, k - 1], s3_s.at[u, k - 1], s3_r.at[u, k - 1], ring[axis][1][k])

    def last_send(unit):
        for k in (2, 1, 3):
            last_put(unit, k).start()

    def last_sum(unit):
        b, p = unit
        u = number(unit)
        base, hi, lo = corner(b)
        for k in (1, 2, 3):
            last_put(unit, k).wait_recv()
        total = last_part(unit, 0)[...].astype(F32)
        for k in range(3):
            total = total + r3[u, k].astype(F32)
        tile = total.astype(BF)
        done[unit][lo] = tile
        for k in (2, 1, 3):
            share(unit, k).start()
        value = tile.astype(F32)
        mean = jnp.sum(value * value, keepdims=True) * (1.0 / (VT * VT))
        squares[c, z, y, 2 * b + p:2 * b + p + 1, :] = jnp.broadcast_to(mean, (1, 128))

    def share(unit, k):
        u = number(unit)
        lo = corner(unit[0])[2]
        return remote(
            done[unit].at[lo], done[unit].at[lo], ag_s.at[u, k - 1], ag_r.at[u, k - 1], ring[MINOR[unit[0]]][1][k]
        )

    def packed(unit, k):
        return r1.at[number(unit), 0, 0, k]

    def deliver(unit, k):
        b, p = unit
        u = number(unit)
        cell = spread.at[c, p, 4 * b + corner(b)[1]]
        if k == 0:
            return pltpu.make_async_copy(packed(unit, 0), cell, st_s.at[u])
        return remote(packed(unit, k), cell, aa_s.at[u, k - 1], aa_r.at[u, k - 1], ring[MAJOR[b]][1][k])

    def handout(unit):
        b, p = unit
        for k in (1, 2, 3):
            share(unit, k).wait_recv()
        for k in (2, 1, 3, 0):
            r1[number(unit), 0, 0, k] = done[unit][plan[2, 4 * b + k]]
            deliver(unit, k).start()

    def core_copy(unit):
        b, p = unit
        rows = spread.at[c, p, 4 * b:4 * b + 4]
        return remote(rows, rows, co_s.at[number(unit)], co_r.at[number(unit)], partner)

    def finish(unit):
        deliver(unit, 0).wait()
        for k in (1, 2, 3):
            deliver(unit, k).wait_recv()
        core_copy(unit).start()

    def phases(unit):
        bind = functools.partial
        if unit in X_FIRST:
            first = [bind(f, unit) for f in (x_begin, x_pass, x_sum, x2_sum)]
        else:
            acts = (m_begin, m_pass, m_sum, m2_sum)
            first = [[bind(f, unit, s) for f in acts] for s in (0, 1)]
        return first, [bind(f, unit) for f in (last_sum, handout, finish)]

    def norms_z(k):
        part = squares.at[c, z, y]
        return remote(part, part, nz_s.at[k - 1], nz_r.at[k - 1], ring["z"][1][k])

    def norms_y(k):
        part = squares.at[c, :, y]
        return remote(part, part, ny_s.at[k - 1], ny_r.at[k - 1], ring["y"][1][k])

    def norms_core():
        return remote(squares.at[c], norms.at[c], nc_s, nc_r, partner)

    def norms_keep():
        return pltpu.make_async_copy(squares.at[c], norms.at[c], nl_s)

    def norms_begin():
        for k in (1, 2, 3):
            norms_z(k).start()

    def norms_next():
        for k in (1, 2, 3):
            norms_z(k).wait_recv()
        for k in (1, 2, 3):
            norms_y(k).start()

    def norms_last():
        for k in (1, 2, 3):
            norms_y(k).wait_recv()
        norms_core().start()
        norms_keep().start()

    events = []
    for unit in UNITS:
        b, p = unit
        first, rest = phases(unit)
        if unit in X_FIRST:
            when = X_WHEN[unit]
            last = when[-1]
            events += list(zip(when, first))
        else:
            for s in (0, 1):
                start = 8 * p + 4 * s + b
                when = [start + n * M_GAP for n in range(4)]
                if start + M_GAP > 15:
                    when = [start] + [max(16, start) + n for n in range(3)]
                else:
                    when = [w if w <= 15 else 16 + n - [v <= 15 for v in when].count(True) for n, w in enumerate(when)]
                last = when[-1]
                events += list(zip(when, first[s]))
        for act in rest:
            last = last + REST_GAP if last + REST_GAP <= 15 else max(16, last + 1)
            events.append((last, act))
    end = max(when for when, act in events)
    norm_at = end - 2
    events += [(norm_at + n, act) for n, act in enumerate((norms_begin, norms_next, norms_last))]
    events = sorted(enumerate(events), key=lambda e: (e[1][0], e[0]))
    by_slot = {}
    for _, (when, act) in events:
        by_slot.setdefault(when, []).append(act)

    def step(s, _):
        @pl.when(s > 0)
        def _():
            amplitude_pairs(s, (0,))

        amplitude_pairs(s, (1, 2))
        amplitude_last(s)
        for b in range(4):
            compute(s, b)
            for k in range(4):
                acts = by_slot.get(4 * k + b, [])
                if acts:
                    @pl.when(s == k)
                    def _():
                        for act in acts:
                            act()
        return 0

    lax.fori_loop(0, 4, step, 0)
    for when in sorted(by_slot):
        if when > 15:
            for act in by_slot[when]:
                act()

    for unit in UNITS:
        core_copy(unit).wait_recv()
    norms_keep().wait()
    norms_core().wait_recv()

    def wait_exchange(i, _):
        exchange(i).wait_send()
        return 0

    lax.fori_loop(0, NC, wait_exchange, 0)
    for unit in UNITS:
        for way in (0, 1):
            for kind in range(3):
                if unit in X_FIRST:
                    x_put(unit, way, kind).wait_send()
                else:
                    for s in (0, 1):
                        for slot in (0, 1):
                            m_put(unit, s, slot, way, kind).wait_send()
        for k in (1, 2, 3):
            if unit in X_FIRST:
                x2_put(unit, k).wait_send()
            else:
                for s in (0, 1):
                    m2_put(unit, s, k).wait_send()
            last_put(unit, k).wait_send()
            share(unit, k).wait_send()
            deliver(unit, k).wait_send()
        core_copy(unit).wait_send()
    for k in (1, 2, 3):
        norms_z(k).wait_send()
        norms_y(k).wait_send()
    norms_core().wait_send()


def ladders(plan, t2_window, factors):
    dma = pltpu.SemaphoreType.DMA
    any_space = pl.BlockSpec(memory_space=pl.ANY)
    smem = pl.BlockSpec(memory_space=pltpu.SMEM)
    vmem = pl.BlockSpec(memory_space=pltpu.VMEM)
    flops = 2 * FILLED * 8 * VT * VT * KC
    spread, norms, _ = pl.pallas_call(
        ladder_kernel,
        out_shape=(
            jax.ShapeDtypeStruct((2, 2, 16, VT, VT), BF),
            jax.ShapeDtypeStruct((2, 4, 4, 8, 128), F32),
            jax.ShapeDtypeStruct(factors.shape, BF),
        ),
        in_specs=[smem, vmem, any_space],
        out_specs=(any_space, any_space, any_space),
        scratch_shapes=[
            pltpu.VMEM((4, 512, 256), BF),
            pltpu.VMEM((53, 256, 256), BF),
            pltpu.VMEM((NC, VT, KC), BF),
            pltpu.VMEM((NC, KC, 256), BF),
            pltpu.VMEM((4, 2, FILLED, VT, VT), BF),
            pltpu.VMEM((2, 3, ROWS, W * VT), BF),
            pltpu.VMEM((8, 2, 3, 8, VT, VT), BF),
            pltpu.VMEM((8, 3, 4, VT, VT), BF),
            pltpu.VMEM((8, 3, VT, VT), BF),
        ]
        + [pltpu.VMEM((4, VT, VT), BF) for _ in UNITS]
        + [
            pltpu.VMEM((2, 4, 4, 8, 128), F32),
            dma((NC,)), dma((NC,)), dma((2, 3)),
            dma((8, 2, 3, 4)), dma((8, 2, 3, 4)), dma((8, 3, 2)), dma((8, 3, 2)), dma((8, 3)), dma((8, 3)),
            dma((8, 3)), dma((8, 3)), dma((8, 3)), dma((8, 3)), dma((8,)), dma((8,)), dma((8,)),
            dma((3,)), dma((3,)), dma((3,)), dma((3,)), dma, dma, dma,
        ],
        compiler_params=pltpu.CompilerParams(
            collective_id=0, has_side_effects=True, vmem_limit_bytes=63 * 2**20
        ),
        cost_estimate=pl.CostEstimate(flops=flops, bytes_accessed=2**24, transcendentals=0),
    )(plan, t2_window, factors)
    return spread, norms


def home_kernel(plan, tiles, norms, residual, out, norms_out, wide):
    s = pl.program_id(0)
    for p in range(4):
        wide[p * 128:p * 128 + 128, :] = tiles[p // 2, p % 2, 0].astype(F32)
    keep = plan[4, s] == 1
    for a in range(VT):
        lanes = slice(a * 128, a * 128 + 128)
        ladder = wide[pl.ds(a, 4, stride=128), :]
        total = residual[0, :, lanes].astype(F32) + ladder
        out[0, :, lanes] = jnp.where(keep, total, 0.0).astype(BF)

    @pl.when(s == 0)
    def _():
        for i in range(2):
            for p in range(4):
                row = norms[pl.ds((p // 2) * 128 + plan[5, i] + p % 2, 1), :]
                norms_out[i, p] = jnp.max(row)


def at_home(plan, spread, norms, residual):
    return pl.pallas_call(
        home_kernel,
        out_shape=(
            jax.ShapeDtypeStruct(residual.shape, BF),
            jax.ShapeDtypeStruct((2, 4), F32),
        ),
        grid_spec=pltpu.PrefetchScalarGridSpec(
            num_scalar_prefetch=1,
            grid=(8,),
            in_specs=[
                pl.BlockSpec((2, 2, 1, VT, VT), lambda s, plan: (0, 0, plan[3, s], 0, 0)),
                pl.BlockSpec((256, 128), lambda s, plan: (0, 0)),
                pl.BlockSpec((1, 4, VT * VT), lambda s, plan: (s, 0, 0)),
            ],
            out_specs=[
                pl.BlockSpec((1, 4, VT * VT), lambda s, plan: (s, 0, 0)),
                pl.BlockSpec(memory_space=pltpu.SMEM),
            ],
            scratch_shapes=[pltpu.VMEM((4 * VT, VT), F32)],
        ),
    )(plan, spread, norms.reshape(256, 128), residual)


def plan_kernel(rows, plan):
    x, y, z, c = place()
    w = lax.axis_index("wide")
    n = 256
    r = lax.broadcasted_iota(I32, (n, n), 0)
    l = lax.broadcasted_iota(I32, (n, n), 1)
    eye = r == l

    def column(v):
        return jnp.sum(jnp.where(eye, v, 0), axis=1, keepdims=True)

    def pick(mask, v):
        return jnp.sum(jnp.where(mask, v, 0), axis=0, keepdims=True)

    mask_row, owner_row, home_row = rows[0:1, :], rows[1:2, :], rows[2:3, :]
    filled, home, owner = column(mask_row) == 1, column(home_row), column(owner_row)
    before = (mask_row == 1) & (home_row < home)
    where = jnp.sum(jnp.where(before, 1, 0), axis=1, keepdims=True)
    cell, turn = where & 15, where >> 4
    index = cell * 4 + turn
    match = filled & (index == l)
    ids = lax.broadcasted_iota(I32, (n, 1), 0)
    first_of = (ids * 4370) >> 16
    plan[0:1, :] = pick(match, first_of)
    plan[1:2, :] = pick(match, ids - first_of * NC)
    chips = pick(match, home >> 4)
    r16 = lax.broadcasted_iota(I32, (16, n), 0)
    t16 = lax.broadcasted_iota(I32, (16, n), 1)
    batch, k = r16 >> 2, r16 & 3
    by_y = (batch & 1) == 0
    group = jnp.where(by_y, y, z)
    far = (group + k) & 3
    target = jnp.where(by_y, z * 4 + far, far * 4 + y)
    hit = (t16 < FILLED) & ((t16 >> 4) == batch) & (((t16 >> 2) & 3) == group) & (chips == target)
    choice = jnp.sum(jnp.where(hit, t16 & 3, 0), axis=1, keepdims=True)
    plan[2:3, :] = pick(r16 == t16, choice)
    here = filled & (home == w * 8 + l) & (l < 8)
    plan[3:4, :] = pick(here, cell)
    plan[4:5, :] = pick(here, 1)
    batch_of, group_of = cell >> 2, cell & 3
    chip_of = jnp.where((batch_of & 1) == 0, turn * 4 + group_of, group_of * 4 + turn)
    plan[5:6, :] = pick(filled & (owner == w * 2 + l) & (l < 2), chip_of * 8 + 2 * batch_of)
    plan[6:8, :] = jnp.zeros((2, n), I32)


def make_plan(tile_mask, owner_slot, home_slot):
    rows = jnp.pad(jnp.stack([tile_mask, owner_slot, home_slot]), ((0, 5), (0, 256 - NT)))
    return pl.pallas_call(plan_kernel, out_shape=jax.ShapeDtypeStruct((8, 256), I32))(rows)


def body(factors, t2_window, residual_in, tile_mask, owner_slot, home_slot):
    plan = make_plan(tile_mask, owner_slot, home_slot)
    spread, norms = ladders(plan, t2_window, factors)
    return at_home(plan, spread, norms, residual_in)


def solution(mesh):
    in_specs = (P(None, ("wide", "narrow"), None), P(), P("wide", "narrow", None), P(), P(), P())
    out_specs = (P("wide", "narrow", None), P("wide", "narrow"))
    return jax.shard_map(body, mesh=mesh, in_specs=in_specs, out_specs=out_specs, check_vma=False)
```
